512 devices in a mesh: row: 16 (over x_hi, y, core), col: 32 (over x_lo, z).
Axes of the slice: x: 4 (x_hi: 2, x_lo: 2; x = x_hi * 2 + x_lo), y: 4, z: 16, core: 2. Of those that a mesh axis runs over, the one named last changes fastest.
Arguments:
- gradient: bfloat16 [4096, 4096], P('row', 'col'), may hold values from -6 to 6
- left_basis: bfloat16 [4096, 4096], P('col', 'row'), may hold values from -0.09375 to 0.09375
- right_basis: bfloat16 [4096, 4096], P('row', 'col'), may hold values from -0.09375 to 0.09375
- first_moment: float32 [4096, 4096], P('row', 'col'), may hold values from -1.8 to 1.8
- second_moment: float32 [4096, 4096], P('row', 'col'), may hold values from 0.05 to 2
- weight: float32 [4096, 4096], P('row', 'col'), may hold values from -0.18 to 0.18
Outputs:
- new_weight: float32 [4096, 4096], P('row', 'col')
- update: bfloat16 [4096, 4096], P('row', 'col')
- new_first: float32 [4096, 4096], P('row', 'col')
- new_second: float32 [4096, 4096], P('row', 'col')
The draws below stay inside these ranges and needn't reach their ends.
All inputs are finite; a program needn't handle non-finite values.
Results may differ from the reference program's by a relative error of at most 0.034.
Values may be sent and summed in bfloat16 or wider, within the bound.
A program may use at most 64 MiB of HBM per device.

```python
import math
import jax
import jax.numpy as jnp
from jax import lax

BLK = 4096
N_ROW = 16
N_COL = 32


def steps_of(rng, extent, shards, low, largest):
    level = 1.0
    for dim, shards_of in shards:
        draws = jax.random.uniform(jax.random.fold_in(jax.random.fold_in(rng, 6), dim), (shards_of,), jnp.float32, low / len(shards), largest / len(shards))
        level = level * jnp.repeat(jnp.exp(draws), extent[dim] // shards_of).reshape((-1,) + (1,) * (len(extent) - 1 - dim))
    return level


def centred(rng, dims, spread, reach, split=(), held_as=jnp.bfloat16):
    drawn = jax.random.normal(rng, dims, jnp.float32) * spread
    if len(split) > 0:
        drawn = steps_of(rng, dims, split, -0.22, 0.18) * drawn
    return jnp.clip(drawn, min=-reach, max=reach).astype(held_as)


def setup_inputs(seed: int = 0) -> dict:
    key_of = jax.random.split(jax.random.key(seed), 7)
    gradient = centred(key_of[0], (BLK, BLK), 1.0, 6.0, ((0, 16), (1, 32)))
    left_basis = centred(key_of[1], (BLK, BLK), BLK ** -0.5, 0.09375, ((0, 32), (1, 16)))
    right_basis = centred(key_of[2], (BLK, BLK), BLK ** -0.5, 0.09375, ((0, 16), (1, 32)))
    first_moment = centred(key_of[3], (BLK, BLK), 0.3, 1.8, ((0, 16), (1, 32)), jnp.float32)
    second_moment = jnp.clip(jnp.exp(math.log(2.0) - 3.6888794 * jax.random.uniform(key_of[4], (BLK, BLK), jnp.float32) ** steps_of(key_of[4], (BLK, BLK), ((0, 16), (1, 32)), -0.2, 0.2)), 0.05, 2.0)
    weight = centred(key_of[5], (BLK, BLK), 0.03, 0.18, ((0, 16), (1, 32)), jnp.float32)
    return dict(gradient=gradient, left_basis=left_basis, right_basis=right_basis, first_moment=first_moment, second_moment=second_moment, weight=weight)


beta_one = 0.9
beta_two = 0.95
epsilon = 1e-08
learn_rate = 0.0003
weight_decay = 0.1
step_count = 20.0

def reference(gradient, left_basis, right_basis, first_moment, second_moment, weight):
    half_rotated = jnp.dot(left_basis.T, gradient, preferred_element_type=jnp.float32).astype(jnp.bfloat16)
    rotated = jnp.dot(half_rotated, right_basis, preferred_element_type=jnp.float32)
    new_first = beta_one * first_moment + (1.0 - beta_one) * rotated
    new_second = beta_two * second_moment + (1.0 - beta_two) * rotated * rotated
    first_hat = new_first / (1.0 - beta_one ** step_count)
    second_hat = new_second / (1.0 - beta_two ** step_count)
    normed = (first_hat / (jnp.sqrt(second_hat) + epsilon)).astype(jnp.bfloat16)
    col_width = BLK // N_COL
    row_width = BLK // N_ROW

    def right_block(total, index):
        start = (index * col_width).astype(jnp.int32)
        cols = lax.dynamic_slice_in_dim(normed, start, col_width, 1)
        basis = lax.dynamic_slice_in_dim(right_basis, start, col_width, 1)
        term = jnp.dot(cols, basis.T, preferred_element_type=jnp.float32).astype(jnp.bfloat16)
        term = lax.optimization_barrier(term)
        return (total + term.astype(jnp.float32), None)
    back_total, _ = lax.scan(right_block, jnp.zeros((BLK, BLK), jnp.float32), jnp.arange(N_COL, dtype=jnp.int32))
    back_half = back_total.astype(jnp.bfloat16)

    def left_block(total, index):
        start = (index * row_width).astype(jnp.int32)
        basis = lax.dynamic_slice_in_dim(left_basis, start, row_width, 1)
        rows = lax.dynamic_slice_in_dim(back_half, start, row_width, 0)
        term = jnp.dot(basis, rows, preferred_element_type=jnp.float32).astype(jnp.bfloat16)
        term = lax.optimization_barrier(term)
        return (total + term.astype(jnp.float32), None)
    full_update, _ = lax.scan(left_block, jnp.zeros((BLK, BLK), jnp.float32), jnp.arange(N_ROW, dtype=jnp.int32))
    update = full_update.astype(jnp.bfloat16)
    new_weight = weight - learn_rate * (full_update + weight_decay * weight)
    return (new_weight, update, new_first, new_second)
```

```python
import functools

import jax
import jax.numpy as jnp
from jax import lax
from jax.experimental import pallas as pl
from jax.experimental.pallas import tpu as pltpu
from jax.sharding import PartitionSpec as P

beta_one = 0.9
beta_two = 0.95
epsilon = 1e-08
learn_rate = 0.0003
weight_decay = 0.1
step_count = 20.0

MESH = pl.DeviceIdType.MESH
CHUNKS = 2


def dot(left, right, left_dim, right_dim):
    return lax.dot_general(
        left,
        right,
        (((left_dim,), (right_dim,)), ((), ())),
        preferred_element_type=jnp.float32,
    )


def kernel(
    ny, nz, tr, tc,
    g_ref, l_ref, r_ref, m1_ref, m2_ref, w_ref,
    nw_ref, up_ref, nf_ref, ns_ref,
    gbuf, lbuf, lsib, rbuf, pbuf, ptile, xsend, xrecv, nbuf, qsend, qrecv, qfull,
    us_up, ur_up, us_dn, ur_dn,
    g_us, g_ur, g_ds, g_dr, l_us, l_ur, l_ds, l_dr, u_us, u_ur, u_ds, u_dr,
    rs_sem, rr_sem, rsib_s, rsib_r, ps_sem, pr_sem, psib_s, psib_r,
    qs_sem, qr_sem, lsib_s, lsib_r, x_s, x_r, n_s, n_r,
):
    bf16 = jnp.bfloat16
    ratio = tr // tc
    steps_up, steps_dn = nz // 2, nz - 1 - nz // 2
    row, col = lax.axis_index("row"), lax.axis_index("col")
    x_hi, y, c = lax.div(row, 2 * ny), lax.rem(lax.div(row, 2), ny), lax.rem(row, 2)
    x_lo, z = lax.div(col, nz), lax.rem(col, nz)
    sib = 1 - c
    diagonal = x_hi == x_lo

    def device(x_hi, y, c, x_lo, z):
        return ((x_hi * ny + y) * 2 + c, x_lo * nz + z)

    above = device(x_hi, y, c, x_lo, lax.rem(z + 1, nz))
    below = device(x_hi, y, c, x_lo, lax.rem(z + nz - 1, nz))
    sibling = device(x_hi, y, sib, x_lo, z)
    beside = device(x_hi, y, c, 1 - x_lo, z)
    beside_sib = device(x_hi, y, sib, 1 - x_lo, z)

    def copy(src, dst, send, recv, to):
        return pltpu.make_async_remote_copy(
            src_ref=src, dst_ref=dst, send_sem=send, recv_sem=recv,
            device_id=to, device_id_type=MESH,
        )

    def loop(n, body):
        lax.fori_loop(0, n, lambda i, carry: (body(i), carry)[1], 0)

    barrier = pltpu.get_barrier_semaphore()

    def greet(to):
        pl.semaphore_signal(barrier, inc=1, device_id=to, device_id_type=MESH)

    def greet_plane(i):
        peer_x, peer_y = lax.div(i, ny), lax.rem(i, ny)
        hi, lo = lax.div(peer_x, 2), lax.rem(peer_x, 2)
        pl.when(~((hi == x_hi) & (lo == x_lo) & (peer_y == y)))(
            lambda: greet(device(hi, peer_y, c, lo, z))
        )

    for to in (above, below, sibling, beside_sib):
        greet(to)
    loop(4 * ny, greet_plane)
    pl.semaphore_wait(barrier, 4 * ny - 1 + 4)

    def ring(buf, us, ur, ds, dr):
        rows = buf.shape[1] // CHUNKS

        def part(tile, ch):
            return buf.at[tile, pl.ds(ch * rows, rows)]

        def up(s, ch, sent):
            tile = lax.rem(z - s + 2 * nz - (0 if sent else 1), nz)
            return copy(part(tile, ch), part(tile, ch), us.at[ch, s], ur.at[ch, s], above)

        def down(s, ch, sent):
            tile = lax.rem(z + s + (0 if sent else 1), nz)
            return copy(part(tile, ch), part(tile, ch), ds.at[ch, s], dr.at[ch, s], below)

        def start():
            for ch in range(CHUNKS):
                up(0, ch, True).start()
                down(0, ch, True).start()

        def middle(s):
            for ch in range(CHUNKS):
                up(s - 1, ch, False).wait_recv()
                up(s, ch, True).start()
                down(s - 1, ch, False).wait_recv()
                down(s, ch, True).start()

        def last():
            for ch in range(CHUNKS):
                up(steps_up - 2, ch, False).wait_recv()
                up(steps_up - 1, ch, True).start()

        def finish():
            for ch in range(CHUNKS):
                down(steps_dn - 1, ch, False).wait_recv()
            for ch in range(CHUNKS):
                up(steps_up - 1, ch, False).wait_recv()

        def sent():
            def one(s):
                for ch in range(CHUNKS):
                    up(s, ch, True).wait_send()

            def two(s):
                for ch in range(CHUNKS):
                    down(s, ch, True).wait_send()

            loop(steps_up, one)
            loop(steps_dn, two)

        return start, middle, last, finish, sent

    def plane(buf, tile, ss, rs, sib_s, sib_r):
        mine = buf.at[x_lo, y * 2 + c]

        def out(i):
            hi, dy = lax.div(i, ny), lax.rem(i, ny)
            is_self = diagonal & (hi == x_hi) & (dy == 0)
            to = device(hi, lax.rem(y + dy, ny), c, x_hi, z)
            return is_self, copy(tile, mine, ss.at[hi, dy], rs.at[x_lo, y], to)

        def start():
            def one(i):
                is_self, send = out(i)
                pl.when(~is_self)(send.start)

            loop(2 * ny, one)

            @pl.when(diagonal)
            def _():
                mine[...] = tile[...]

        def forward(i, own):
            jj, ys = lax.div(i, ny), lax.rem(i, ny)
            slot = buf.at[jj, ys * 2 + (c if own else sib)]
            return jj, ys, slot, copy(slot, slot, sib_s.at[jj, ys], sib_r.at[jj, ys], sibling)

        def relay():
            def one(i):
                jj, ys, slot, send = forward(i, True)
                is_self = diagonal & (jj == x_lo) & (ys == y)
                pl.when(~is_self)(
                    copy(tile, slot, ss.at[0, 0], rs.at[jj, ys], sibling).wait_recv
                )
                send.start()

            loop(2 * ny, one)

        def finish():
            loop(2 * ny, lambda i: forward(i, False)[3].wait_recv())

        def sent():
            def one(i):
                is_self, send = out(i)
                pl.when(~is_self)(send.wait_send)
                forward(i, True)[3].wait_send()

            loop(2 * ny, one)

        return start, relay, finish, sent

    g_start, g_middle, g_last, g_finish, g_sent = ring(gbuf, g_us, g_ur, g_ds, g_dr)
    l_start, l_middle, l_last, l_finish, l_sent = ring(lbuf, l_us, l_ur, l_ds, l_dr)
    r_start, r_relay, r_finish, r_sent = plane(rbuf, r_ref, rs_sem, rr_sem, rsib_s, rsib_r)
    p_start, p_relay, p_finish, p_sent = plane(pbuf, ptile, ps_sem, pr_sem, psib_s, psib_r)

    def swap_start(which, partial):
        first, second = partial[:, :tc], partial[:, tc:]
        xsend[which] = jnp.where(x_lo == 0, second, first).astype(bf16)
        swap(which).start()
        return jnp.where(x_lo == 0, first, second)

    def swap(which):
        return copy(xsend.at[which], xrecv.at[which], x_s.at[which], x_r.at[which], beside)

    gbuf[z] = g_ref[...]
    lbuf[z] = l_ref[...]
    g_start()
    r_start()
    lax.fori_loop(1, steps_up // 2, lambda s, carry: (g_middle(s), carry)[1], 0)
    r_relay()
    lax.fori_loop(steps_up // 2, steps_dn, lambda s, carry: (g_middle(s), carry)[1], 0)
    g_last()
    l_start()
    r_finish()
    g_finish()

    partial = jnp.zeros((tr, 2 * tc), jnp.float32)
    for b in range(2 * ny):
        left = jnp.concatenate([gbuf[b * ratio + k] for k in range(ratio)], axis=1)
        right = jnp.concatenate([rbuf[0, b], rbuf[1, b]], axis=1)
        partial += dot(left, right, 1, 0)
    mine = swap_start(0, partial)
    ptile_f32 = mine
    if steps_dn > 1:
        l_middle(1)
    swap(0).wait_recv()
    ptile[...] = (ptile_f32 + xrecv[0].astype(jnp.float32)).astype(bf16)
    p_start()
    lax.fori_loop(2, steps_dn, lambda s, carry: (l_middle(s), carry)[1], 0)
    l_last()
    p_relay()
    l_finish()

    def share_l(yy):
        rows = pl.ds((2 * yy + sib) * ratio, ratio)
        return copy(lbuf.at[rows], lsib.at[yy], lsib_s.at[yy], lsib_r.at[yy], sibling)

    loop(ny, lambda yy: share_l(yy).start())
    p_finish()

    partial = jnp.zeros((tr, 2 * tc), jnp.float32)
    for b in range(2 * ny):
        left = lbuf[b * ratio : (b + 1) * ratio].reshape(tr, tr)
        right = jnp.concatenate([pbuf[0, b], pbuf[1, b]], axis=1)
        partial += dot(left, right, 0, 0)
    mine = swap_start(1, partial)
    swap(1).wait_recv()
    rotated = mine + xrecv[1].astype(jnp.float32)
    new_first = beta_one * m1_ref[...] + (1.0 - beta_one) * rotated
    new_second = beta_two * m2_ref[...] + (1.0 - beta_two) * rotated * rotated
    nf_ref[...] = new_first
    ns_ref[...] = new_second
    first_hat = new_first / (1.0 - beta_one**step_count)
    second_hat = new_second / (1.0 - beta_two**step_count)
    nbuf[c, x_lo] = (first_hat / (jnp.sqrt(second_hat) + epsilon)).astype(bf16)

    def share_n(k, to, core, lo):
        slot = nbuf.at[core, lo]
        return copy(nbuf.at[c, x_lo], slot, n_s.at[k], n_r.at[k], to)

    targets = (beside, sibling, beside_sib)
    sources = ((c, 1 - x_lo), (sib, x_lo), (sib, 1 - x_lo))
    for k in range(3):
        share_n(k, targets[k], c, x_lo).start()
    loop(ny, lambda yy: share_l(yy).wait_recv())
    for k in range(3):
        share_n(k, targets[k], *sources[k]).wait_recv()

    def q_out(yy, jj):
        is_self = diagonal & (jj == x_lo) & (yy == y)
        to = device(x_lo, yy, c, jj, z)
        return is_self, copy(
            qsend.at[jj, yy], qrecv.at[x_hi, y], qs_sem.at[jj, yy], qr_sem.at[x_hi, y], to
        )

    own_n = jnp.concatenate([nbuf[c, 0], nbuf[c, 1]], axis=1)
    sib_n = jnp.concatenate([nbuf[sib, 0], nbuf[sib, 1]], axis=1)
    for yy in range(ny):
        own_l = lbuf[pl.ds((2 * yy + c) * ratio, ratio)].reshape(tr, tr)
        sib_l = lsib[yy].reshape(tr, tr)
        block = (dot(own_l, own_n, 1, 0) + dot(sib_l, sib_n, 1, 0)).astype(bf16)
        for jj in range(2):
            qsend[jj, yy] = block[:, jj * tc : (jj + 1) * tc]
            is_self, send = q_out(yy, jj)
            pl.when(~is_self)(send.start)

    @pl.when(diagonal)
    def _():
        qrecv[x_hi, y] = qsend[x_lo, y]

    total = jnp.zeros((tr, tc), jnp.float32)
    for hi in range(2):
        for yy in range(ny):
            is_self = diagonal & (hi == x_hi) & (yy == y)
            pl.when(~is_self)(
                copy(ptile, qrecv.at[hi, yy], qs_sem.at[0, 0], qr_sem.at[hi, yy], beside).wait_recv
            )
            total += qrecv[hi, yy].astype(jnp.float32)
    qfull[x_lo] = total.astype(bf16)

    def share_q(lo):
        return copy(qfull.at[x_lo], qfull.at[lo], x_s.at[2], x_r.at[2], beside)

    share_q(x_lo).start()
    share_q(1 - x_lo).wait_recv()

    def tile_of(d):
        d = lax.rem(d + 2 * nz, nz)
        rows = pl.ds(lax.rem(d, ratio) * tc, tc)
        at = lax.div(d, ratio)
        left = jnp.concatenate([qfull[0], qfull[1]], axis=1)
        right = jnp.concatenate([rbuf[0, at, rows], rbuf[1, at, rows]], axis=1)
        return dot(left, right, 1, 1)

    def u_up(s):
        return copy(us_up.at[s], ur_up.at[s], u_us.at[s], u_ur.at[s], above)

    def u_down(s):
        return copy(us_dn.at[s], ur_dn.at[s], u_ds.at[s], u_dr.at[s], below)

    us_up[0] = tile_of(z + steps_up).astype(bf16)
    u_up(0).start()
    us_dn[0] = tile_of(z - steps_dn).astype(bf16)
    u_down(0).start()

    def up_step(s):
        term = tile_of(z + steps_up - s)
        u_up(s - 1).wait_recv()
        us_up[s] = (term + ur_up[s - 1].astype(jnp.float32)).astype(bf16)
        u_up(s).start()

    def u_step(s):
        up_step(s)
        term = tile_of(z - steps_dn + s)
        u_down(s - 1).wait_recv()
        us_dn[s] = (term + ur_dn[s - 1].astype(jnp.float32)).astype(bf16)
        u_down(s).start()

    lax.fori_loop(1, steps_dn, lambda s, carry: (u_step(s), carry)[1], 0)
    up_step(steps_up - 1)
    full = tile_of(z)
    u_down(steps_dn - 1).wait_recv()
    full += ur_dn[steps_dn - 1].astype(jnp.float32)
    u_up(steps_up - 1).wait_recv()
    full += ur_up[steps_up - 1].astype(jnp.float32)
    weight = w_ref[...]
    up_ref[...] = full.astype(bf16)
    nw_ref[...] = weight - learn_rate * (full + weight_decay * weight)

    g_sent()
    l_sent()
    r_sent()
    p_sent()
    for which in range(2):
        swap(which).wait_send()
    share_q(x_lo).wait_send()
    loop(ny, lambda yy: share_l(yy).wait_send())
    for k in range(3):
        share_n(k, targets[k], c, x_lo).wait_send()

    def q_sent(i):
        is_self, send = q_out(lax.rem(i, ny), lax.div(i, ny))
        pl.when(~is_self)(send.wait_send)

    loop(2 * ny, q_sent)
    loop(steps_up, lambda s: u_up(s).wait_send())
    loop(steps_dn, lambda s: u_down(s).wait_send())


def on_device(n_row, n_col, gradient, left_basis, right_basis, first_moment, second_moment, weight):
    ny, nz = n_row // 4, n_col // 2
    tr, tc = gradient.shape
    up, dn = nz // 2, nz - 1 - nz // 2
    bf16 = jnp.bfloat16
    ratio = tr // tc
    dma = pltpu.SemaphoreType.DMA
    ring = [dma((CHUNKS, up)), dma((CHUNKS, up)), dma((CHUNKS, dn)), dma((CHUNKS, dn))]
    f32_tile = jax.ShapeDtypeStruct((tr, tc), jnp.float32)
    vmem = pl.BlockSpec(memory_space=pltpu.VMEM)
    return pl.pallas_call(
        functools.partial(kernel, ny, nz, tr, tc),
        out_shape=[f32_tile, jax.ShapeDtypeStruct((tr, tc), bf16), f32_tile, f32_tile],
        in_specs=[vmem] * 6,
        out_specs=[vmem] * 4,
        scratch_shapes=[
            pltpu.VMEM((nz, tr, tc), bf16),
            pltpu.VMEM((nz, tc, tr), bf16),
            pltpu.VMEM((ny, ratio, tc, tr), bf16),
            pltpu.VMEM((2, 2 * ny, tr, tc), bf16),
            pltpu.VMEM((2, 2 * ny, tr, tc), bf16),
            pltpu.VMEM((tr, tc), bf16),
            pltpu.VMEM((2, tr, tc), bf16),
            pltpu.VMEM((2, tr, tc), bf16),
            pltpu.VMEM((2, 2, tr, tc), bf16),
            pltpu.VMEM((2, ny, tr, tc), bf16),
            pltpu.VMEM((2, ny, tr, tc), bf16),
            pltpu.VMEM((2, tr, tc), bf16),
            pltpu.VMEM((up, tr, tc), bf16),
            pltpu.VMEM((up, tr, tc), bf16),
            pltpu.VMEM((dn, tr, tc), bf16),
            pltpu.VMEM((dn, tr, tc), bf16),
        ]
        + ring
        + ring
        + [dma((up,)), dma((up,)), dma((dn,)), dma((dn,))]
        + [dma((2, ny))] * 10
        + [dma((ny,)), dma((ny,)), dma((3,)), dma((3,)), dma((3,)), dma((3,))],
        compiler_params=pltpu.CompilerParams(
            collective_id=0, has_side_effects=True, vmem_limit_bytes=40 * 2**20
        ),
    )(gradient, left_basis, right_basis, first_moment, second_moment, weight)


def solution(mesh):
    spec = P("row", "col")
    return jax.shard_map(
        functools.partial(on_device, mesh.shape["row"], mesh.shape["col"]),
        mesh=mesh,
        in_specs=(spec, P("col", "row"), spec, spec, spec, spec),
        out_specs=(spec,) * 4,
        check_vma=False,
    )
```

```python
import functools

import jax
import jax.numpy as jnp
from jax import lax
from jax.experimental import pallas as pl
from jax.experimental.pallas import tpu as pltpu
from jax.sharding import PartitionSpec as P

beta_one = 0.9
beta_two = 0.95
epsilon = 1e-08
learn_rate = 0.0003
weight_decay = 0.1
step_count = 20.0

MESH = pl.DeviceIdType.MESH
G_HOP, L_HOP, U_HOP = 1, 1, 2
L_PARTS = 2


def dot(left, right, left_dim, right_dim):
    return lax.dot_general(
        left,
        right,
        (((left_dim,), (right_dim,)), ((), ())),
        preferred_element_type=jnp.float32,
    )


def loop(n, body):
    lax.fori_loop(0, n, lambda i, carry: (body(i), carry)[1], 0)


def copy(src, dst, send, recv, to):
    return pltpu.make_async_remote_copy(
        src_ref=src, dst_ref=dst, send_sem=send, recv_sem=recv,
        device_id=to, device_id_type=MESH,
    )


def hops(distance, hop):
    return [hop] * (distance // hop) + ([distance % hop] if distance % hop else [])


class Gather:
    def __init__(self, z, nz, sign, hop, distance, pieces, part, first, send, recv, at):
        self.z, self.nz, self.sign, self.pieces = z, nz, sign, pieces
        self.part, self.first, self.send, self.recv, self.at = part, first, send, recv, at
        self.hops = hops(distance, hop)
        self.stops = [sum(self.hops[:k]) for k in range(len(self.hops) + 1)]

    def piece(self, k, off, ch, sender):
        i = self.stops[k] + off - 1
        away = self.stops[k] + (0 if sender else off)
        tile = self.part(lax.rem(self.z - self.sign * away + 2 * self.nz, self.nz), ch)
        src, dst, other = tile, tile, False
        if k == 0 and sender:
            src, dst, other = self.first(ch)
        to = self.at(lax.rem(self.z + self.sign * off + self.nz, self.nz), other)
        return copy(src, dst, self.send.at[ch, i], self.recv.at[ch, i], to)

    def step(self, k, ch):
        if k < len(self.hops):
            if k > 0:
                self.piece(k - 1, self.hops[k - 1], ch, False).wait_recv()
            for off in range(self.hops[k], 0, -1):
                self.piece(k, off, ch, True).start()

    def finish(self):
        last = len(self.hops) - 1
        for k, hop in enumerate(self.hops):
            for off in range(1, hop + (k == last)):
                for ch in range(self.pieces):
                    self.piece(k, off, ch, False).wait_recv()

    def sent(self):
        for k, hop in enumerate(self.hops):
            for off in range(1, hop + 1):
                for ch in range(self.pieces):
                    self.piece(k, off, ch, True).wait_send()


class Scatter:
    def __init__(self, z, nz, sign, hop, distance, own, out, into, send, recv, at):
        self.z, self.nz, self.sign = z, nz, sign
        self.own, self.out, self.into, self.send, self.recv, self.at = own, out, into, send, recv, at
        self.hops = hops(distance, hop)
        self.stops = [sum(self.hops[:k]) for k in range(len(self.hops) + 1)]

    def piece(self, k, off, ch):
        i = self.stops[k] + off - 1
        to = self.at(lax.rem(self.z + self.sign * off + self.nz, self.nz), k == 0 and ch == 1)
        return copy(self.out.at[ch, i], self.into.at[ch, i], self.send.at[ch, i], self.recv.at[ch, i], to)

    def arrived(self, k, ch, total):
        if k < len(self.hops):
            for off in range(1, self.hops[k] + 1):
                self.piece(k, off, ch).wait_recv()
                total += self.into[ch, self.stops[k] + off - 1].astype(jnp.float32)
        return total

    def far(self, k, ch):
        if k < len(self.hops):
            stop = self.stops[k + 1]
            total = self.arrived(k + 1, ch, self.own(self.sign * stop, ch))
            self.out[ch, stop - 1] = total.astype(jnp.bfloat16)
            self.piece(k, self.hops[k], ch).start()

    def near(self, k, ch):
        if k < len(self.hops):
            for off in range(1, self.hops[k]):
                stop = self.stops[k] + off
                self.out[ch, stop - 1] = self.own(self.sign * stop, ch).astype(jnp.bfloat16)
                self.piece(k, off, ch).start()

    def sent(self):
        for k, hop in enumerate(self.hops):
            for off in range(1, hop + 1):
                for ch in range(2):
                    self.piece(k, off, ch).wait_send()


def kernel(
    ny, nz, tr, tc,
    g_hbm, l_hbm, r_hbm, m1_hbm, m2_hbm, w_hbm,
    nw_hbm, up_hbm, nf_hbm, ns_hbm,
    g_ref, m1_ref, m2_ref, w_ref, nw_ref, up_ref, nf_ref, ns_ref,
    gbuf, lbuf, lsib, rbuf, ptile, pbuf, xsend, xrecv, nbuf, qsend, qrecv,
    uo_up, ui_up, uo_dn, ui_dn, uo_x, ui_x,
    in_sem, out_sem,
    g_us, g_ur, g_ds, g_dr, l_us, l_ur, l_ds, l_dr, u_us, u_ur, u_ds, u_dr,
    r_s, r_r, rsib_s, rsib_r, p_s, p_r, psib_s, psib_r, q_s, q_r,
    lsib_s, lsib_r, x_s, x_r, n_s, n_r,
):
    bf16 = jnp.bfloat16
    ratio, hr = tr // tc, tr // 2
    far_up, far_dn = nz // 2, nz - 1 - nz // 2
    row, col = lax.axis_index("row"), lax.axis_index("col")
    x_hi, y, c = lax.div(row, 2 * ny), lax.rem(lax.div(row, 2), ny), lax.rem(row, 2)
    x_lo, z = lax.div(col, nz), lax.rem(col, nz)
    sib = 1 - c
    diagonal = x_hi == x_lo

    own_r = rbuf.at[x_hi, x_lo, y * 2 + c]
    sources = (g_hbm, l_hbm, r_hbm, m1_hbm, m2_hbm, w_hbm)
    places = (g_ref, lbuf.at[z], own_r, m1_ref, m2_ref, w_ref)
    loads = [pltpu.make_async_copy(s, d, in_sem.at[i]) for i, (s, d) in enumerate(zip(sources, places))]
    for load in loads:
        load.start()

    def device(x_hi, y, c, x_lo, z):
        return ((x_hi * ny + y) * 2 + c, x_lo * nz + z)

    def along(to_z, other):
        return device(x_hi, y, c, 1 - x_lo if other else x_lo, to_z)

    sibling = device(x_hi, y, sib, x_lo, z)
    beside = device(x_hi, y, c, 1 - x_lo, z)
    beside_sib = device(x_hi, y, sib, 1 - x_lo, z)

    barrier = pltpu.get_barrier_semaphore()

    def greet(to):
        pl.semaphore_signal(barrier, inc=1, device_id=to, device_id_type=MESH)

    def in_plane(i):
        peer = lax.rem(x_hi * 2 + x_lo + lax.div(i, ny), 4)
        return lax.div(peer, 2), lax.rem(peer, 2), lax.rem(y + lax.rem(i, ny), ny)

    def greet_plane(i):
        hi, lo, yy = in_plane(i + 1)
        greet(device(hi, yy, c, lo, z))

    near = sorted({k % nz for k in (1, -1, 2, -2)} - {0})
    for k in near:
        for other in (False, True):
            greet(along(lax.rem(z + k, nz), other))
    greet(sibling)
    greet(beside_sib)
    loop(4 * ny - 1, greet_plane)
    pl.semaphore_wait(barrier, 2 * len(near) + 2 + 4 * ny - 1)

    def g_part(tile, ch):
        return gbuf.at[x_lo if ch == 0 else 1 - x_lo, tile]

    def g_half(which):
        return g_ref.at[pl.ds(pl.multiple_of(which * hr, hr), hr)]

    def g_first(ch):
        return g_half(x_lo if ch == 0 else 1 - x_lo), gbuf.at[x_lo, z], ch == 1

    lrows = tc // L_PARTS

    def l_part(tile, ch):
        return lbuf.at[tile, pl.ds(ch * lrows, lrows)]

    def l_first(ch):
        return l_part(z, ch), l_part(z, ch), False

    g_rings = [
        Gather(z, nz, 1, G_HOP, far_up, 2, g_part, g_first, g_us, g_ur, along),
        Gather(z, nz, -1, G_HOP, far_dn, 2, g_part, g_first, g_ds, g_dr, along),
    ]
    l_rings = [
        Gather(z, nz, 1, L_HOP, far_up, L_PARTS, l_part, l_first, l_us, l_ur, along),
        Gather(z, nz, -1, L_HOP, far_dn, L_PARTS, l_part, l_first, l_ds, l_dr, along),
    ]

    pending = [ring.sent for ring in g_rings + l_rings]

    def ring_step(rings, k):
        for ch in range(rings[0].pieces):
            for ring in rings:
                ring.step(k, ch)

    def g_beside():
        return copy(g_half(1 - x_lo), gbuf.at[x_lo, z], x_s.at[0], x_r.at[0], beside)

    def r_out(i):
        hi, lo, yy = in_plane(i)
        return copy(
            own_r, own_r, r_s.at[i], r_r.at[x_hi * 2 + x_lo, y], device(hi, yy, c, lo, z)
        )

    def r_relay(i, own):
        hi, lo, yy = in_plane(i)
        slot = rbuf.at[hi, lo, yy * 2 + (c if own else sib)]
        at = (hi * 2 + lo, yy)
        send = copy(slot, slot, rsib_s.at[at], rsib_r.at[at], sibling)
        arrive = copy(slot, slot, r_s.at[0], r_r.at[at], sibling)
        return arrive, send

    def r_pass(i):
        arrive, send = r_relay(i, True)
        arrive.wait_recv()
        send.start()

    loads[0].wait()
    g_ref_ready = pl.ds(pl.multiple_of(x_lo * hr, hr), hr)
    gbuf[x_lo, z] = g_ref[g_ref_ready, :]
    ring_step(g_rings, 0)
    g_beside().start()
    loads[1].wait()
    ring_step(l_rings, 0)
    loads[2].wait()
    loop(4 * ny - 1, lambda i: r_out(i + 1).start())
    r_relay(0, True)[1].start()

    pending.append(g_beside().wait_send)
    pending.append(lambda: loop(4 * ny - 1, lambda i: r_out(i + 1).wait_send()))
    pending.append(lambda: loop(4 * ny, lambda i: r_relay(i, True)[1].wait_send()))
    g_steps, l_steps = len(g_rings[0].hops), len(l_rings[0].hops)
    relayed, rounds = 1, max(g_steps, l_steps)
    for k in range(1, rounds):
        ring_step(g_rings, k)
        ring_step(l_rings, k)
        if k >= rounds // 2:
            left = rounds - k
            upto = relayed + (4 * ny - relayed + left - 1) // left
            lax.fori_loop(relayed, upto, lambda i, carry: (r_pass(i), carry)[1], 0)
            relayed = upto
    lax.fori_loop(relayed, 4 * ny, lambda i, carry: (r_pass(i), carry)[1], 0)
    loop(4 * ny, lambda i: r_relay(i, False)[1].wait_recv())
    for ring in g_rings:
        ring.finish()
    g_beside().wait_recv()

    partial = jnp.zeros((hr, 2 * tc), jnp.float32)
    for hi in range(2):
        for b in range(2 * ny):
            left = jnp.concatenate([gbuf[hi, b * ratio + k] for k in range(ratio)], axis=1)
            right = jnp.concatenate([rbuf[hi, 0, b], rbuf[hi, 1, b]], axis=1)
            partial += dot(left, right, 1, 0)
    ptile[...] = partial.astype(bf16)

    own_p = pbuf.at[y * 2 + c, x_lo]

    def p_out(i):
        hi, dy = lax.div(i, ny), lax.rem(i, ny)
        is_self = diagonal & (hi == x_hi) & (dy == 0)
        to = device(hi, lax.rem(y + dy, ny), c, x_hi, z)
        return is_self, copy(ptile, own_p, p_s.at[hi, dy], p_r.at[x_lo, y], to)

    def p_start(i):
        is_self, send = p_out(i)
        pl.when(~is_self)(send.start)

    loop(2 * ny, p_start)

    def p_sent(i):
        is_self, send = p_out(i)
        pl.when(~is_self)(send.wait_send)

    pending.append(lambda: loop(2 * ny, p_sent))

    @pl.when(diagonal)
    def _():
        pbuf[y * 2 + c, x_lo] = ptile[...]

    for ring in l_rings:
        ring.finish()

    def share_l(yy):
        rows = pl.ds((2 * yy + sib) * ratio, ratio)
        return copy(lbuf.at[rows], lsib.at[yy], lsib_s.at[yy], lsib_r.at[yy], sibling)

    def p_relay(dy, lo, own):
        yy = lax.rem(y + dy, ny)
        slot = pbuf.at[yy * 2 + (c if own else sib), lo]
        is_self = diagonal & (lo == x_lo) & (dy == 0)
        arrive = copy(ptile, slot, p_s.at[0, 0], p_r.at[lo, yy], sibling)
        return is_self, arrive, copy(slot, slot, psib_s.at[lo, yy], psib_r.at[lo, yy], sibling)

    partial = jnp.zeros((tr, 2 * tc), jnp.float32)

    def rotate(partial, dy, core):
        block = lax.rem(y + dy, ny) * 2 + core
        left = lbuf[pl.ds(block * ratio, ratio)].reshape(tr, tr)
        return partial + dot(left, pbuf[block].reshape(tr, 2 * tc), 0, 0)

    for dy in range(ny):
        for lo in range(2):
            is_self, arrive, send = p_relay(dy, lo, True)
            pl.when(~is_self)(arrive.wait_recv)
            send.start()
        partial = rotate(partial, dy, c)
    for dy in range(ny):
        for lo in range(2):
            p_relay(dy, lo, False)[2].wait_recv()
        partial = rotate(partial, dy, sib)

    pending.append(
        lambda: loop(2 * ny, lambda i: p_relay(lax.rem(i, ny), lax.div(i, ny), True)[2].wait_send())
    )
    first, second = partial[:, :tc], partial[:, tc:]
    xsend[...] = jnp.where(x_lo == 0, second, first).astype(bf16)
    swap = copy(xsend, xrecv, x_s.at[1], x_r.at[1], beside)
    swap.start()
    loop(ny, lambda yy: share_l(yy).start())
    for load in loads[3:]:
        load.wait()
    mine = jnp.where(x_lo == 0, first, second)
    swap.wait_recv()
    pending.append(swap.wait_send)
    pending.append(lambda: loop(ny, lambda yy: share_l(yy).wait_send()))
    rotated = mine + xrecv[...].astype(jnp.float32)
    new_first = beta_one * m1_ref[...] + (1.0 - beta_one) * rotated
    new_second = beta_two * m2_ref[...] + (1.0 - beta_two) * rotated * rotated
    first_hat = new_first / (1.0 - beta_one**step_count)
    second_hat = new_second / (1.0 - beta_two**step_count)
    nbuf[c, x_lo] = (first_hat / (jnp.sqrt(second_hat) + epsilon)).astype(bf16)

    def share_n(k, to, core, lo):
        slot = nbuf.at[core, lo]
        return copy(nbuf.at[c, x_lo], slot, n_s.at[k], n_r.at[k], to)

    targets = (beside, beside_sib, sibling)
    origins = ((c, 1 - x_lo), (sib, 1 - x_lo), (sib, x_lo))
    for k in range(3):
        share_n(k, targets[k], c, x_lo).start()
    nf_ref[...] = new_first
    ns_ref[...] = new_second
    saves = [
        pltpu.make_async_copy(s, d, out_sem.at[i])
        for i, (s, d) in enumerate(
            ((nf_ref, nf_hbm), (ns_ref, ns_hbm), (nw_ref, nw_hbm), (up_ref, up_hbm))
        )
    ]
    saves[0].start()
    saves[1].start()
    pending += [saves[0].wait, saves[1].wait]
    loop(ny, lambda yy: share_l(yy).wait_recv())
    for k in range(3):
        share_n(k, targets[k], *origins[k]).wait_recv()
        pending.append(share_n(k, targets[k], c, x_lo).wait_send)

    def q_out(dy, half):
        yy = lax.rem(y + dy, ny)
        is_self = diagonal & (half == x_lo) & (dy == 0)
        to = device(x_lo, yy, c, half, z)
        return is_self, copy(
            qsend.at[dy, half], qrecv.at[x_hi, y], q_s.at[dy, half], q_r.at[x_hi, y], to
        )

    own_n = jnp.concatenate([nbuf[c, 0], nbuf[c, 1]], axis=1)
    sib_n = jnp.concatenate([nbuf[sib, 0], nbuf[sib, 1]], axis=1)
    for step in range(ny):
        dy = (step + 1) % ny
        yy = lax.rem(y + dy, ny)
        own_l = lbuf[pl.ds((2 * yy + c) * ratio, ratio)].reshape(tr, tr)
        sib_l = lsib[yy].reshape(tr, tr)
        block = (dot(own_l, own_n, 1, 0) + dot(sib_l, sib_n, 1, 0)).astype(bf16)
        for half in range(2):
            qsend[dy, half] = block[half * hr : (half + 1) * hr]
            is_self, send = q_out(dy, half)
            pl.when(~is_self)(send.start)

    @pl.when(diagonal)
    def _():
        qrecv[x_hi, y] = qsend[0, x_lo]

    total = jnp.zeros((hr, 2 * tc), jnp.float32)
    for dy in range(ny):
        yy = lax.rem(y + dy, ny)
        for hi in range(2):
            is_self = diagonal & (hi == x_hi) & (dy == 0)
            arrive = copy(ptile, qrecv.at[hi, yy], q_s.at[0, 0], q_r.at[hi, yy], beside)
            pl.when(~is_self)(arrive.wait_recv)
            total += qrecv[hi, yy].astype(jnp.float32)
    q = total.astype(bf16)

    def q_sent(i):
        is_self, send = q_out(lax.rem(i, ny), lax.div(i, ny))
        pl.when(~is_self)(send.wait_send)

    pending.append(lambda: loop(2 * ny, q_sent))

    def u_own(away, ch):
        d = lax.rem(z + away + nz, nz)
        hi = x_lo if ch == 0 else 1 - x_lo
        rows = pl.ds(pl.multiple_of(lax.rem(d, ratio) * tc, tc), tc)
        at = lax.div(d, ratio)
        right = jnp.concatenate([rbuf[hi, 0, at, rows], rbuf[hi, 1, at, rows]], axis=1)
        return dot(q, right, 1, 1)

    u_rings = [
        Scatter(z, nz, 1, U_HOP, far_up, u_own, uo_up, ui_up, u_us, u_ur, along),
        Scatter(z, nz, -1, U_HOP, far_dn, u_own, uo_dn, ui_dn, u_ds, u_dr, along),
    ]
    u_beside = copy(uo_x, ui_x, x_s.at[2], x_r.at[2], beside)
    for k in reversed(range(len(u_rings[0].hops))):
        for ch in (1, 0):
            for ring in u_rings:
                ring.far(k, ch)
            for ring in u_rings:
                ring.near(k, ch)
        if k == len(u_rings[0].hops) - 1:
            uo_x[...] = u_own(0, 1).astype(bf16)
            u_beside.start()

    def finish(which, total, ch):
        for ring in u_rings:
            total = ring.arrived(0, ch, total)
        rows = pl.ds(pl.multiple_of(which * hr, hr), hr)
        weight = w_ref[rows, :]
        up_ref[rows, :] = total.astype(bf16)
        nw_ref[rows, :] = weight - learn_rate * (total + weight_decay * weight)

    mine = u_own(0, 0)
    u_beside.wait_recv()
    finish(1 - x_lo, ui_x[...].astype(jnp.float32), 1)
    finish(x_lo, mine, 0)
    saves[2].start()
    saves[3].start()
    pending += [saves[2].wait, saves[3].wait, u_beside.wait_send]
    pending += [ring.sent for ring in u_rings]

    for wait in pending:
        wait()


def on_device(n_row, n_col, gradient, left_basis, right_basis, first_moment, second_moment, weight):
    ny, nz = n_row // 4, n_col // 2
    tr, tc = gradient.shape
    up, dn = nz // 2, nz - 1 - nz // 2
    bf16, f32 = jnp.bfloat16, jnp.float32
    ratio, hr = tr // tc, tr // 2
    dma = pltpu.SemaphoreType.DMA
    f32_tile = jax.ShapeDtypeStruct((tr, tc), f32)
    anywhere = pl.BlockSpec(memory_space=pl.ANY)

    def ring(pieces):
        return [dma((pieces, up)), dma((pieces, up)), dma((pieces, dn)), dma((pieces, dn))]

    return pl.pallas_call(
        functools.partial(kernel, ny, nz, tr, tc),
        out_shape=[f32_tile, jax.ShapeDtypeStruct((tr, tc), bf16), f32_tile, f32_tile],
        in_specs=[anywhere] * 6,
        out_specs=[anywhere] * 4,
        scratch_shapes=[
            pltpu.VMEM((tr, tc), bf16),
            pltpu.VMEM((tr, tc), f32),
            pltpu.VMEM((tr, tc), f32),
            pltpu.VMEM((tr, tc), f32),
            pltpu.VMEM((tr, tc), f32),
            pltpu.VMEM((tr, tc), bf16),
            pltpu.VMEM((tr, tc), f32),
            pltpu.VMEM((tr, tc), f32),
            pltpu.VMEM((2, nz, hr, tc), bf16),
            pltpu.VMEM((nz, tc, tr), bf16),
            pltpu.VMEM((ny, ratio, tc, tr), bf16),
            pltpu.VMEM((2, 2, 2 * ny, tr, tc), bf16),
            pltpu.VMEM((hr, 2 * tc), bf16),
            pltpu.VMEM((2 * ny, 2, hr, 2 * tc), bf16),
            pltpu.VMEM((tr, tc), bf16),
            pltpu.VMEM((tr, tc), bf16),
            pltpu.VMEM((2, 2, tr, tc), bf16),
            pltpu.VMEM((ny, 2, hr, 2 * tc), bf16),
            pltpu.VMEM((2, ny, hr, 2 * tc), bf16),
            pltpu.VMEM((2, up, hr, tc), bf16),
            pltpu.VMEM((2, up, hr, tc), bf16),
            pltpu.VMEM((2, dn, hr, tc), bf16),
            pltpu.VMEM((2, dn, hr, tc), bf16),
            pltpu.VMEM((hr, tc), bf16),
            pltpu.VMEM((hr, tc), bf16),
            dma((6,)),
            dma((4,)),
        ]
        + ring(2)
        + ring(L_PARTS)
        + ring(2)
        + [dma((4 * ny,)), dma((4, ny)), dma((4, ny)), dma((4, ny))]
        + [dma((2, ny))] * 4
        + [dma((ny, 2)), dma((2, ny))]
        + [dma((ny,)), dma((ny,)), dma((3,)), dma((3,)), dma((3,)), dma((3,))],
        compiler_params=pltpu.CompilerParams(
            collective_id=0, has_side_effects=True, vmem_limit_bytes=60 * 2**20
        ),
    )(gradient, left_basis, right_basis, first_moment, second_moment, weight)


def solution(mesh):
    spec = P("row", "col")
    return jax.shard_map(
        functools.partial(on_device, mesh.shape["row"], mesh.shape["col"]),
        mesh=mesh,
        in_specs=(spec, P("col", "row"), spec, spec, spec, spec),
        out_specs=(spec,) * 4,
        check_vma=False,
    )
```

```python
import functools

import jax
import jax.numpy as jnp
from jax import lax
from jax.experimental import pallas as pl
from jax.experimental.pallas import tpu as pltpu
from jax.sharding import PartitionSpec as P

beta_one = 0.9
beta_two = 0.95
epsilon = 1e-08
learn_rate = 0.0003
weight_decay = 0.1
step_count = 20.0

MESH = pl.DeviceIdType.MESH
G_UP, G_DN = (2, 2, 1, 1, 1, 1), (2, 2, 1, 1, 1)
L_UP, L_DN = (1, 1, 1, 1, 1, 1, 1, 1), (1, 1, 1, 1, 1, 1, 1)
U_UP, U_DN = (2, 2, 2, 2), (2, 2, 2, 1)
LAG = 1
PARTS = 2
RELAY_AT = 5
L_PARTS = 2


def dot(left, right, left_dim, right_dim):
    return lax.dot_general(
        left,
        right,
        (((left_dim,), (right_dim,)), ((), ())),
        preferred_element_type=jnp.float32,
    )


def loop(n, body):
    lax.fori_loop(0, n, lambda i, carry: (body(i), carry)[1], 0)


def copy(src, dst, send, recv, to):
    return pltpu.make_async_remote_copy(
        src_ref=src, dst_ref=dst, send_sem=send, recv_sem=recv,
        device_id=to, device_id_type=MESH,
    )


def hops(distance, wanted):
    out = []
    for hop in wanted:
        out.append(min(hop, distance - sum(out)))
    return [hop for hop in out if hop > 0]


class Gather:
    def __init__(self, z, nz, sign, hop, distance, pieces, part, first, send, recv, at):
        self.z, self.nz, self.sign, self.pieces = z, nz, sign, pieces
        self.part, self.first, self.send, self.recv, self.at = part, first, send, recv, at
        self.hops = hops(distance, hop)
        self.stops = [sum(self.hops[:k]) for k in range(len(self.hops) + 1)]

    def piece(self, k, off, ch, sender):
        i = self.stops[k] + off - 1
        away = self.stops[k] + (0 if sender else off)
        tile = self.part(lax.rem(self.z - self.sign * away + 2 * self.nz, self.nz), ch)
        src, dst, other = tile, tile, False
        if k == 0 and sender:
            src, dst, other = self.first(ch)
        to = self.at(lax.rem(self.z + self.sign * off + self.nz, self.nz), other)
        return copy(src, dst, self.send.at[ch, i], self.recv.at[ch, i], to)

    def step(self, k, ch):
        if k < len(self.hops):
            if k > 0:
                self.piece(k - 1, self.hops[k - 1], ch, False).wait_recv()
            for off in range(self.hops[k], 0, -1):
                self.piece(k, off, ch, True).start()

    def finish(self):
        last = len(self.hops) - 1
        for k, hop in enumerate(self.hops):
            for off in range(1, hop + (k == last)):
                for ch in range(self.pieces):
                    self.piece(k, off, ch, False).wait_recv()

    def sent(self):
        for k, hop in enumerate(self.hops):
            for off in range(1, hop + 1):
                for ch in range(self.pieces):
                    self.piece(k, off, ch, True).wait_send()


class Scatter:
    def __init__(self, z, nz, sign, hop, distance, own, out, into, send, recv, at):
        self.z, self.nz, self.sign = z, nz, sign
        self.own, self.out, self.into, self.send, self.recv, self.at = own, out, into, send, recv, at
        self.hops = hops(distance, hop)
        self.stops = [sum(self.hops[:k]) for k in range(len(self.hops) + 1)]

    def piece(self, k, off, ch):
        i = self.stops[k] + off - 1
        to = self.at(lax.rem(self.z + self.sign * off + self.nz, self.nz), k == 0 and ch % 2 == 1)
        return copy(self.out.at[ch, i], self.into.at[ch, i], self.send.at[ch, i], self.recv.at[ch, i], to)

    def arrived(self, k, ch, total):
        if k < len(self.hops):
            for off in range(1, self.hops[k] + 1):
                self.piece(k, off, ch).wait_recv()
                total += self.into[ch, self.stops[k] + off - 1].astype(jnp.float32)
        return total

    def far(self, k, ch):
        if k < len(self.hops):
            stop = self.stops[k + 1]
            total = self.arrived(k + 1, ch, self.own(self.sign * stop, ch))
            self.out[ch, stop - 1] = total.astype(jnp.bfloat16)
            self.piece(k, self.hops[k], ch).start()

    def near(self, k, ch):
        if k < len(self.hops):
            for off in range(1, self.hops[k]):
                stop = self.stops[k] + off
                self.out[ch, stop - 1] = self.own(self.sign * stop, ch).astype(jnp.bfloat16)
                self.piece(k, off, ch).start()

    def sent(self):
        for k, hop in enumerate(self.hops):
            for off in range(1, hop + 1):
                for ch in range(2 * PARTS):
                    self.piece(k, off, ch).wait_send()


def kernel(
    ny, nz, tr, tc,
    g_hbm, l_hbm, r_hbm, m1_hbm, m2_hbm,
    full_hbm, rot_hbm,
    g_ref, m1_ref, m2_ref, full_ref, rot_ref,
    gbuf, lbuf, lsib, rbuf, ptile, pbuf, xsend, xrecv, nbuf, qsend, qrecv,
    uo_up, ui_up, uo_dn, ui_dn, uo_x, ui_x,
    in_sem, out_sem,
    g_us, g_ur, g_ds, g_dr, l_us, l_ur, l_ds, l_dr, u_us, u_ur, u_ds, u_dr,
    r_s, r_r, rsib_s, rsib_r, p_s, p_r, psib_s, psib_r, q_s, q_r,
    lsib_s, lsib_r, x_s, x_r, n_s, n_r,
):
    bf16 = jnp.bfloat16
    ratio, hr = tr // tc, tr // 2
    hp = hr // PARTS
    far_up, far_dn = nz // 2, nz - 1 - nz // 2
    row, col = lax.axis_index("row"), lax.axis_index("col")
    x_hi, y, c = lax.div(row, 2 * ny), lax.rem(lax.div(row, 2), ny), lax.rem(row, 2)
    x_lo, z = lax.div(col, nz), lax.rem(col, nz)
    sib = 1 - c
    diagonal = x_hi == x_lo

    own_r = rbuf.at[x_hi, x_lo, y * 2 + c]
    sources = (g_hbm, l_hbm, r_hbm, m1_hbm, m2_hbm)
    places = (g_ref, lbuf.at[z], own_r, m1_ref, m2_ref)
    loads = [pltpu.make_async_copy(s, d, in_sem.at[i]) for i, (s, d) in enumerate(zip(sources, places))]
    for load in loads:
        load.start()

    def device(x_hi, y, c, x_lo, z):
        return ((x_hi * ny + y) * 2 + c, x_lo * nz + z)

    def along(to_z, other):
        return device(x_hi, y, c, 1 - x_lo if other else x_lo, to_z)

    sibling = device(x_hi, y, sib, x_lo, z)
    beside = device(x_hi, y, c, 1 - x_lo, z)
    beside_sib = device(x_hi, y, sib, 1 - x_lo, z)

    barrier = pltpu.get_barrier_semaphore()

    def greet(to):
        pl.semaphore_signal(barrier, inc=1, device_id=to, device_id_type=MESH)

    def in_plane(i):
        peer = lax.rem(x_hi * 2 + x_lo + lax.div(i, ny), 4)
        return lax.div(peer, 2), lax.rem(peer, 2), lax.rem(y + lax.rem(i, ny), ny)

    def greet_plane(i):
        hi, lo, yy = in_plane(i + 1)
        greet(device(hi, yy, c, lo, z))

    near = sorted({k % nz for k in (1, -1, 2, -2)} - {0})
    for k in near:
        for other in (False, True):
            greet(along(lax.rem(z + k, nz), other))
    greet(sibling)
    greet(beside_sib)
    loop(4 * ny - 1, greet_plane)
    pl.semaphore_wait(barrier, 2 * len(near) + 2 + 4 * ny - 1)

    def g_part(tile, ch):
        return gbuf.at[x_lo if ch == 0 else 1 - x_lo, tile]

    def g_half(which):
        return g_ref.at[pl.ds(pl.multiple_of(which * hr, hr), hr)]

    def g_first(ch):
        return g_half(x_lo if ch == 0 else 1 - x_lo), gbuf.at[x_lo, z], ch == 1

    lrows = tc // L_PARTS

    def l_part(tile, ch):
        return lbuf.at[tile, pl.ds(ch * lrows, lrows)]

    def l_first(ch):
        return l_part(z, ch), l_part(z, ch), False

    g_rings = [
        Gather(z, nz, 1, G_UP, far_up, 2, g_part, g_first, g_us, g_ur, along),
        Gather(z, nz, -1, G_DN, far_dn, 2, g_part, g_first, g_ds, g_dr, along),
    ]
    l_rings = [
        Gather(z, nz, 1, L_UP, far_up, L_PARTS, l_part, l_first, l_us, l_ur, along),
        Gather(z, nz, -1, L_DN, far_dn, L_PARTS, l_part, l_first, l_ds, l_dr, along),
    ]

    pending = [ring.sent for ring in g_rings + l_rings]

    def ring_step(rings, k):
        for ch in range(rings[0].pieces):
            for ring in rings:
                ring.step(k, ch)

    def g_beside():
        return copy(g_half(1 - x_lo), gbuf.at[x_lo, z], x_s.at[0], x_r.at[0], beside)

    def r_out(i):
        hi, lo, yy = in_plane(i)
        return copy(
            own_r, own_r, r_s.at[i], r_r.at[x_hi * 2 + x_lo, y], device(hi, yy, c, lo, z)
        )

    def r_relay(i, own):
        hi, lo, yy = in_plane(i)
        slot = rbuf.at[hi, lo, yy * 2 + (c if own else sib)]
        at = (hi * 2 + lo, yy)
        send = copy(slot, slot, rsib_s.at[at], rsib_r.at[at], sibling)
        arrive = copy(slot, slot, r_s.at[0], r_r.at[at], sibling)
        return arrive, send

    def r_pass(i):
        arrive, send = r_relay(i, True)
        arrive.wait_recv()
        send.start()

    loads[0].wait()
    g_ref_ready = pl.ds(pl.multiple_of(x_lo * hr, hr), hr)
    gbuf[x_lo, z] = g_ref[g_ref_ready, :]
    ring_step(g_rings, 0)
    g_beside().start()
    loads[1].wait()
    loads[2].wait()
    loop(4 * ny - 1, lambda i: r_out(i + 1).start())
    r_relay(0, True)[1].start()
    pending.append(g_beside().wait_send)
    pending.append(lambda: loop(4 * ny - 1, lambda i: r_out(i + 1).wait_send()))
    pending.append(lambda: loop(4 * ny, lambda i: r_relay(i, True)[1].wait_send()))

    g_steps, l_steps = len(g_rings[0].hops), len(l_rings[0].hops)
    relayed, l_done = 1, 0
    for k in range(g_steps):
        if k > 0:
            ring_step(g_rings, k)
        if k >= LAG and l_done < l_steps:
            ring_step(l_rings, l_done)
            l_done += 1
        if k >= min(RELAY_AT, g_steps - 1):
            left = g_steps - k
            upto = relayed + (4 * ny - relayed + left - 1) // left
            lax.fori_loop(relayed, upto, lambda i, carry: (r_pass(i), carry)[1], 0)
            relayed = upto
    loop(4 * ny, lambda i: r_relay(i, False)[1].wait_recv())
    for ring in g_rings:
        ring.finish()
    g_beside().wait_recv()

    partial = jnp.zeros((hr, 2 * tc), jnp.float32)
    for hi in range(2):
        for b in range(2 * ny):
            left = jnp.concatenate([gbuf[hi, b * ratio + k] for k in range(ratio)], axis=1)
            right = jnp.concatenate([rbuf[hi, 0, b], rbuf[hi, 1, b]], axis=1)
            partial += dot(left, right, 1, 0)
    ptile[...] = partial.astype(bf16)

    own_p = pbuf.at[y * 2 + c, x_lo]

    def p_out(i):
        hi, dy = lax.div(i, ny), lax.rem(i, ny)
        is_self = diagonal & (hi == x_hi) & (dy == 0)
        to = device(hi, lax.rem(y + dy, ny), c, x_hi, z)
        return is_self, copy(ptile, own_p, p_s.at[hi, dy], p_r.at[x_lo, y], to)

    def p_start(i):
        is_self, send = p_out(i)
        pl.when(~is_self)(send.start)

    loop(2 * ny, p_start)

    def p_sent(i):
        is_self, send = p_out(i)
        pl.when(~is_self)(send.wait_send)

    pending.append(lambda: loop(2 * ny, p_sent))

    @pl.when(diagonal)
    def _():
        pbuf[y * 2 + c, x_lo] = ptile[...]

    for k in range(l_done, l_steps):
        ring_step(l_rings, k)
    for ring in l_rings:
        ring.finish()

    def share_l(yy):
        rows = pl.ds((2 * yy + sib) * ratio, ratio)
        return copy(lbuf.at[rows], lsib.at[yy], lsib_s.at[yy], lsib_r.at[yy], sibling)

    def p_relay(dy, lo, own):
        yy = lax.rem(y + dy, ny)
        slot = pbuf.at[yy * 2 + (c if own else sib), lo]
        is_self = diagonal & (lo == x_lo) & (dy == 0)
        arrive = copy(ptile, slot, p_s.at[0, 0], p_r.at[lo, yy], sibling)
        return is_self, arrive, copy(slot, slot, psib_s.at[lo, yy], psib_r.at[lo, yy], sibling)

    partial = jnp.zeros((tr, 2 * tc), jnp.float32)

    def rotate(partial, dy, core):
        block = lax.rem(y + dy, ny) * 2 + core
        left = lbuf[pl.ds(block * ratio, ratio)].reshape(tr, tr)
        return partial + dot(left, pbuf[block].reshape(tr, 2 * tc), 0, 0)

    for dy in range(ny):
        for lo in range(2):
            is_self, arrive, send = p_relay(dy, lo, True)
            pl.when(~is_self)(arrive.wait_recv)
            send.start()
        partial = rotate(partial, dy, c)
    for dy in range(ny):
        for lo in range(2):
            p_relay(dy, lo, False)[2].wait_recv()
        partial = rotate(partial, dy, sib)

    pending.append(
        lambda: loop(2 * ny, lambda i: p_relay(lax.rem(i, ny), lax.div(i, ny), True)[2].wait_send())
    )
    first, second = partial[:, :tc], partial[:, tc:]
    xsend[...] = jnp.where(x_lo == 0, second, first).astype(bf16)
    swap = copy(xsend, xrecv, x_s.at[1], x_r.at[1], beside)
    swap.start()
    loop(ny, lambda yy: share_l(yy).start())
    for load in loads[3:]:
        load.wait()
    mine = jnp.where(x_lo == 0, first, second)
    swap.wait_recv()
    pending.append(swap.wait_send)
    pending.append(lambda: loop(ny, lambda yy: share_l(yy).wait_send()))
    rotated = mine + xrecv[...].astype(jnp.float32)
    new_first = beta_one * m1_ref[...] + (1.0 - beta_one) * rotated
    new_second = beta_two * m2_ref[...] + (1.0 - beta_two) * rotated * rotated
    first_hat = new_first / (1.0 - beta_one**step_count)
    second_hat = new_second / (1.0 - beta_two**step_count)
    nbuf[c, x_lo] = (first_hat / (jnp.sqrt(second_hat) + epsilon)).astype(bf16)

    def share_n(k, to, core, lo):
        slot = nbuf.at[core, lo]
        return copy(nbuf.at[c, x_lo], slot, n_s.at[k], n_r.at[k], to)

    targets = (beside, beside_sib, sibling)
    origins = ((c, 1 - x_lo), (sib, 1 - x_lo), (sib, x_lo))
    for k in range(3):
        share_n(k, targets[k], c, x_lo).start()
    rot_ref[...] = rotated
    saves = [
        pltpu.make_async_copy(rot_ref, rot_hbm, out_sem.at[0]),
        pltpu.make_async_copy(full_ref, full_hbm, out_sem.at[1]),
    ]
    saves[0].start()
    pending.append(saves[0].wait)
    loop(ny, lambda yy: share_l(yy).wait_recv())
    for k in range(3):
        share_n(k, targets[k], *origins[k]).wait_recv()
        pending.append(share_n(k, targets[k], c, x_lo).wait_send)

    def q_out(dy, half, part):
        yy = lax.rem(y + dy, ny)
        is_self = diagonal & (half == x_lo) & (dy == 0)
        return is_self, copy(
            qsend.at[dy, half, part],
            qrecv.at[x_hi, y, part],
            q_s.at[dy, half, part],
            q_r.at[x_hi, y, part],
            device(x_lo, yy, c, half, z),
        )

    def q_start(dy, half, part):
        is_self, send = q_out(dy, half, part)
        pl.when(~is_self)(send.start)

    own_n = jnp.concatenate([nbuf[c, 0], nbuf[c, 1]], axis=1)
    sib_n = jnp.concatenate([nbuf[sib, 0], nbuf[sib, 1]], axis=1)
    for step in range(ny):
        dy = (step + 1) % ny
        yy = lax.rem(y + dy, ny)
        own_l = lbuf[pl.ds((2 * yy + c) * ratio, ratio)].reshape(tr, tr)
        sib_l = lsib[yy].reshape(tr, tr)
        block = (dot(own_l, own_n, 1, 0) + dot(sib_l, sib_n, 1, 0)).astype(bf16)
        for half in range(2):
            for part in range(PARTS):
                at = half * hr + part * hp
                qsend[dy, half, part] = block[at : at + hp]
            q_start(dy, half, 0)
    for part in range(1, PARTS):
        for step in range(ny):
            for half in range(2):
                q_start((step + 1) % ny, half, part)

    @pl.when(diagonal)
    def _():
        qrecv[x_hi, y] = qsend[0, x_lo]

    def q_sum(part):
        total = jnp.zeros((hp, 2 * tc), jnp.float32)
        for dy in range(ny):
            yy = lax.rem(y + dy, ny)
            for hi in range(2):
                is_self = diagonal & (hi == x_hi) & (dy == 0)
                slot = qrecv.at[hi, yy, part]
                arrive = copy(slot, slot, q_s.at[0, 0, part], q_r.at[hi, yy, part], beside)
                pl.when(~is_self)(arrive.wait_recv)
                total += qrecv[hi, yy, part].astype(jnp.float32)
        return total.astype(bf16)

    def q_sent(i):
        for part in range(PARTS):
            is_self, send = q_out(lax.rem(i, ny), lax.div(i, ny), part)
            pl.when(~is_self)(send.wait_send)

    pending.append(lambda: loop(2 * ny, q_sent))

    q = [None] * PARTS

    def u_own(away, ch):
        d = lax.rem(z + away + nz, nz)
        hi = x_lo if ch % 2 == 0 else 1 - x_lo
        rows = pl.ds(pl.multiple_of(lax.rem(d, ratio) * tc, tc), tc)
        at = lax.div(d, ratio)
        right = jnp.concatenate([rbuf[hi, 0, at, rows], rbuf[hi, 1, at, rows]], axis=1)
        return dot(q[ch // 2], right, 1, 1)

    u_rings = [
        Scatter(z, nz, 1, U_UP, far_up, u_own, uo_up, ui_up, u_us, u_ur, along),
        Scatter(z, nz, -1, U_DN, far_dn, u_own, uo_dn, ui_dn, u_ds, u_dr, along),
    ]

    def u_beside(part):
        return copy(uo_x.at[part], ui_x.at[part], x_s.at[2 + part], x_r.at[2 + part], beside)

    first_step = len(u_rings[0].hops) - 1
    for k in range(first_step, -1, -1):
        for part in range(PARTS):
            if k == first_step:
                q[part] = q_sum(part)
            for ch in (2 * part + 1, 2 * part):
                for ring in u_rings:
                    ring.far(k, ch)
                for ring in u_rings:
                    ring.near(k, ch)
            if k == first_step:
                uo_x[part] = u_own(0, 2 * part + 1).astype(bf16)
                u_beside(part).start()

    for part in range(PARTS):
        own = u_own(0, 2 * part)
        u_beside(part).wait_recv()
        for which, total, ch in (
            (1 - x_lo, ui_x[part].astype(jnp.float32), 2 * part + 1),
            (x_lo, own, 2 * part),
        ):
            for ring in u_rings:
                total = ring.arrived(0, ch, total)
            rows = pl.ds(pl.multiple_of(which * hr + part * hp, hp), hp)
            full_ref[rows, :] = total
        pending.append(u_beside(part).wait_send)
    saves[1].start()
    pending.append(saves[1].wait)
    pending += [ring.sent for ring in u_rings]

    for wait in pending:
        wait()


def on_device(n_row, n_col, gradient, left_basis, right_basis, first_moment, second_moment, weight):
    ny, nz = n_row // 4, n_col // 2
    tr, tc = gradient.shape
    up, dn = nz // 2, nz - 1 - nz // 2
    bf16, f32 = jnp.bfloat16, jnp.float32
    ratio, hr = tr // tc, tr // 2
    hp = hr // PARTS
    dma = pltpu.SemaphoreType.DMA
    f32_tile = jax.ShapeDtypeStruct((tr, tc), f32)
    anywhere = pl.BlockSpec(memory_space=pl.ANY)

    def ring(pieces):
        return [dma((pieces, up)), dma((pieces, up)), dma((pieces, dn)), dma((pieces, dn))]

    full_update, rotated = pl.pallas_call(
        functools.partial(kernel, ny, nz, tr, tc),
        out_shape=[f32_tile, f32_tile],
        in_specs=[anywhere] * 5,
        out_specs=[anywhere] * 2,
        scratch_shapes=[
            pltpu.VMEM((tr, tc), bf16),
            pltpu.VMEM((tr, tc), f32),
            pltpu.VMEM((tr, tc), f32),
            pltpu.VMEM((tr, tc), f32),
            pltpu.VMEM((tr, tc), f32),
            pltpu.VMEM((2, nz, hr, tc), bf16),
            pltpu.VMEM((nz, tc, tr), bf16),
            pltpu.VMEM((ny, ratio, tc, tr), bf16),
            pltpu.VMEM((2, 2, 2 * ny, tr, tc), bf16),
            pltpu.VMEM((hr, 2 * tc), bf16),
            pltpu.VMEM((2 * ny, 2, hr, 2 * tc), bf16),
            pltpu.VMEM((tr, tc), bf16),
            pltpu.VMEM((tr, tc), bf16),
            pltpu.VMEM((2, 2, tr, tc), bf16),
            pltpu.VMEM((ny, 2, PARTS, hp, 2 * tc), bf16),
            pltpu.VMEM((2, ny, PARTS, hp, 2 * tc), bf16),
            pltpu.VMEM((2 * PARTS, up, hp, tc), bf16),
            pltpu.VMEM((2 * PARTS, up, hp, tc), bf16),
            pltpu.VMEM((2 * PARTS, dn, hp, tc), bf16),
            pltpu.VMEM((2 * PARTS, dn, hp, tc), bf16),
            pltpu.VMEM((PARTS, hp, tc), bf16),
            pltpu.VMEM((PARTS, hp, tc), bf16),
            dma((5,)),
            dma((2,)),
        ]
        + ring(2)
        + ring(L_PARTS)
        + ring(2 * PARTS)
        + [dma((4 * ny,)), dma((4, ny)), dma((4, ny)), dma((4, ny))]
        + [dma((2, ny))] * 4
        + [dma((ny, 2, PARTS)), dma((2, ny, PARTS))]
        + [dma((ny,)), dma((ny,)), dma((2 + PARTS,)), dma((2 + PARTS,)), dma((3,)), dma((3,))],
        compiler_params=pltpu.CompilerParams(
            collective_id=0, has_side_effects=True, vmem_limit_bytes=60 * 2**20
        ),
    )(gradient, left_basis, right_basis, first_moment, second_moment)
    new_first = beta_one * first_moment + (1.0 - beta_one) * rotated
    new_second = beta_two * second_moment + (1.0 - beta_two) * rotated * rotated
    update = full_update.astype(bf16)
    new_weight = weight - learn_rate * (full_update + weight_decay * weight)
    return new_weight, update, new_first, new_second


def solution(mesh):
    spec = P("row", "col")
    return jax.shard_map(
        functools.partial(on_device, mesh.shape["row"], mesh.shape["col"]),
        mesh=mesh,
        in_specs=(spec, P("col", "row"), spec, spec, spec, spec),
        out_specs=(spec,) * 4,
        check_vma=False,
    )
```

```python
import functools

import jax
import jax.numpy as jnp
from jax import lax
from jax.experimental import pallas as pl
from jax.experimental.pallas import tpu as pltpu
from jax.sharding import PartitionSpec as P

beta_one = 0.9
beta_two = 0.95
epsilon = 1e-08
learn_rate = 0.0003
weight_decay = 0.1
step_count = 20.0

MESH = pl.DeviceIdType.MESH
G_UP, G_DN = (2, 2, 2, 1, 1), (2, 2, 2, 1)
L_UP, L_DN = (1, 1, 1, 1, 1, 1, 1, 1), (1, 1, 1, 1, 1, 1, 1)
U_UP, U_DN = (2, 2, 2, 2), (2, 2, 2, 1)
LAG = 1
PARTS = 2
G_PARTS = 1
RELAY_AT = 5
L_PARTS = 2


def dot(left, right, left_dim, right_dim):
    return lax.dot_general(
        left,
        right,
        (((left_dim,), (right_dim,)), ((), ())),
        preferred_element_type=jnp.float32,
    )


def loop(n, body):
    lax.fori_loop(0, n, lambda i, carry: (body(i), carry)[1], 0)


def copy(src, dst, send, recv, to):
    return pltpu.make_async_remote_copy(
        src_ref=src, dst_ref=dst, send_sem=send, recv_sem=recv,
        device_id=to, device_id_type=MESH,
    )


def hops(distance, wanted):
    out = []
    for hop in wanted:
        out.append(min(hop, distance - sum(out)))
    return [hop for hop in out if hop > 0]


class Gather:
    def __init__(self, z, nz, sign, hop, distance, pieces, part, first, send, recv, at):
        self.z, self.nz, self.sign, self.pieces = z, nz, sign, tuple(pieces)
        self.part, self.first, self.send, self.recv, self.at = part, first, send, recv, at
        self.hops = hops(distance, hop)
        self.stops = [sum(self.hops[:k]) for k in range(len(self.hops) + 1)]

    def piece(self, k, off, ch, sender):
        i = self.stops[k] + off - 1
        away = self.stops[k] + (0 if sender else off)
        tile = self.part(lax.rem(self.z - self.sign * away + 2 * self.nz, self.nz), ch)
        src, dst, other = tile, tile, False
        if k == 0 and sender:
            src, dst, other = self.first(ch)
        to = self.at(lax.rem(self.z + self.sign * off + self.nz, self.nz), other)
        return copy(src, dst, self.send.at[ch, i], self.recv.at[ch, i], to)

    def step(self, k, ch):
        if k < len(self.hops):
            if k > 0:
                self.piece(k - 1, self.hops[k - 1], ch, False).wait_recv()
            for off in range(self.hops[k], 0, -1):
                self.piece(k, off, ch, True).start()

    def finish(self, pieces):
        last = len(self.hops) - 1
        for k, hop in enumerate(self.hops):
            for off in range(1, hop + (k == last)):
                for ch in self.pieces:
                    if ch in pieces:
                        self.piece(k, off, ch, False).wait_recv()

    def sent(self):
        for k, hop in enumerate(self.hops):
            for off in range(1, hop + 1):
                for ch in self.pieces:
                    self.piece(k, off, ch, True).wait_send()


class Scatter:
    def __init__(self, z, nz, sign, hop, distance, pieces, own, out, into, send, recv, at):
        self.z, self.nz, self.sign, self.pieces = z, nz, sign, tuple(pieces)
        self.own, self.out, self.into, self.send, self.recv, self.at = own, out, into, send, recv, at
        self.hops = hops(distance, hop)
        self.stops = [sum(self.hops[:k]) for k in range(len(self.hops) + 1)]

    def piece(self, k, off, ch):
        i = self.stops[k] + off - 1
        to = self.at(lax.rem(self.z + self.sign * off + self.nz, self.nz), k == 0 and ch % 2 == 1)
        return copy(self.out.at[ch, i], self.into.at[ch, i], self.send.at[ch, i], self.recv.at[ch, i], to)

    def arrived(self, k, ch, total):
        if k < len(self.hops) and ch in self.pieces:
            for off in range(1, self.hops[k] + 1):
                self.piece(k, off, ch).wait_recv()
                total += self.into[ch, self.stops[k] + off - 1].astype(jnp.float32)
        return total

    def far(self, k, ch):
        if k < len(self.hops) and ch in self.pieces:
            stop = self.stops[k + 1]
            total = self.arrived(k + 1, ch, self.own(self.sign * stop, ch))
            self.out[ch, stop - 1] = total.astype(jnp.bfloat16)
            self.piece(k, self.hops[k], ch).start()

    def near(self, k, ch):
        if k < len(self.hops) and ch in self.pieces:
            for off in range(1, self.hops[k]):
                stop = self.stops[k] + off
                self.out[ch, stop - 1] = self.own(self.sign * stop, ch).astype(jnp.bfloat16)
                self.piece(k, off, ch).start()

    def sent(self):
        for k, hop in enumerate(self.hops):
            for off in range(1, hop + 1):
                for ch in self.pieces:
                    self.piece(k, off, ch).wait_send()


def kernel(
    ny, nz, tr, tc,
    g_hbm, l_hbm, r_hbm, m1_hbm, m2_hbm,
    full_hbm, rot_hbm,
    g_ref, m1_ref, m2_ref, full_ref, rot_ref,
    gbuf, lbuf, lsib, rbuf, ptile, pbuf, xsend, xrecv, nbuf, qsend, qrecv,
    uo_up, ui_up, uo_dn, ui_dn, uo_x, ui_x,
    in_sem, out_sem,
    g_us, g_ur, g_ds, g_dr, l_us, l_ur, l_ds, l_dr, u_us, u_ur, u_ds, u_dr,
    r_s, r_r, rsib_s, rsib_r, p_s, p_r, psib_s, psib_r, q_s, q_r,
    lsib_s, lsib_r, x_s, x_r, n_s, n_r,
):
    bf16 = jnp.bfloat16
    ratio, hr = tr // tc, tr // 2
    hp = hr // PARTS
    far_up, far_dn = nz // 2, nz - 1 - nz // 2
    row, col = lax.axis_index("row"), lax.axis_index("col")
    x_hi, y, c = lax.div(row, 2 * ny), lax.rem(lax.div(row, 2), ny), lax.rem(row, 2)
    x_lo, z = lax.div(col, nz), lax.rem(col, nz)
    sib = 1 - c
    diagonal = x_hi == x_lo

    own_r = rbuf.at[x_hi, x_lo, y * 2 + c]
    sources = (g_hbm, l_hbm, r_hbm, m1_hbm, m2_hbm)
    places = (g_ref, lbuf.at[z], own_r, m1_ref, m2_ref)
    loads = [pltpu.make_async_copy(s, d, in_sem.at[i]) for i, (s, d) in enumerate(zip(sources, places))]
    for load in loads:
        load.start()

    def device(x_hi, y, c, x_lo, z):
        return ((x_hi * ny + y) * 2 + c, x_lo * nz + z)

    def along(to_z, other):
        return device(x_hi, y, c, 1 - x_lo if other else x_lo, to_z)

    sibling = device(x_hi, y, sib, x_lo, z)
    beside = device(x_hi, y, c, 1 - x_lo, z)
    beside_sib = device(x_hi, y, sib, 1 - x_lo, z)

    barrier = pltpu.get_barrier_semaphore()

    def greet(to):
        pl.semaphore_signal(barrier, inc=1, device_id=to, device_id_type=MESH)

    def in_plane(i):
        peer = lax.rem(x_hi * 2 + x_lo + lax.div(i, ny), 4)
        return lax.div(peer, 2), lax.rem(peer, 2), lax.rem(y + lax.rem(i, ny), ny)

    def greet_plane(i):
        hi, lo, yy = in_plane(i + 1)
        greet(device(hi, yy, c, lo, z))

    near = sorted({k % nz for k in (1, -1, 2, -2)} - {0})
    for k in near:
        for other in (False, True):
            greet(along(lax.rem(z + k, nz), other))
    greet(sibling)
    greet(beside_sib)
    loop(4 * ny - 1, greet_plane)
    pl.semaphore_wait(barrier, 2 * len(near) + 2 + 4 * ny - 1)

    hg = hr // G_PARTS

    def g_part(tile, ch):
        return gbuf.at[ch // 2, x_lo if ch % 2 == 0 else 1 - x_lo, tile]

    def g_rows(which, part):
        return g_ref.at[pl.ds(pl.multiple_of(which * hr + part * hg, hg), hg)]

    def g_first(ch):
        which = x_lo if ch % 2 == 0 else 1 - x_lo
        return g_rows(which, ch // 2), gbuf.at[ch // 2, x_lo, z], ch % 2 == 1

    lrows = tc // L_PARTS

    def l_part(tile, ch):
        return lbuf.at[tile, pl.ds(ch * lrows, lrows)]

    def l_first(ch):
        return l_part(z, ch), l_part(z, ch), False

    own_g, other_g = range(0, 2 * G_PARTS, 2), range(1, 2 * G_PARTS, 2)
    g_rings = [
        Gather(z, nz, 1, G_UP, far_up, own_g, g_part, g_first, g_us, g_ur, along),
        Gather(z, nz, -1, G_DN, far_dn, own_g, g_part, g_first, g_ds, g_dr, along),
        Gather(z, nz, -1, G_UP, far_up, other_g, g_part, g_first, g_ds, g_dr, along),
        Gather(z, nz, 1, G_DN, far_dn, other_g, g_part, g_first, g_us, g_ur, along),
    ]
    l_all = range(L_PARTS)
    l_rings = [
        Gather(z, nz, 1, L_UP, far_up, l_all, l_part, l_first, l_us, l_ur, along),
        Gather(z, nz, -1, L_DN, far_dn, l_all, l_part, l_first, l_ds, l_dr, along),
    ]

    pending = [ring.sent for ring in g_rings + l_rings]

    def ring_step(rings, k):
        for ch in sorted({ch for ring in rings for ch in ring.pieces}):
            for ring in rings:
                if ch in ring.pieces:
                    ring.step(k, ch)

    def g_beside(part):
        sem = 2 + PARTS + part
        return copy(
            g_rows(1 - x_lo, part), gbuf.at[part, x_lo, z], x_s.at[sem], x_r.at[sem], beside
        )

    def r_out(i):
        hi, lo, yy = in_plane(i)
        return copy(
            own_r, own_r, r_s.at[i], r_r.at[x_hi * 2 + x_lo, y], device(hi, yy, c, lo, z)
        )

    def r_relay(i, own):
        hi, lo, yy = in_plane(i)
        slot = rbuf.at[hi, lo, yy * 2 + (c if own else sib)]
        at = (hi * 2 + lo, yy)
        send = copy(slot, slot, rsib_s.at[at], rsib_r.at[at], sibling)
        arrive = copy(slot, slot, r_s.at[0], r_r.at[at], sibling)
        return arrive, send

    def r_pass(i):
        arrive, send = r_relay(i, True)
        arrive.wait_recv()
        send.start()

    loads[0].wait()
    for part in range(G_PARTS):
        at = pl.ds(pl.multiple_of(x_lo * hr + part * hg, hg), hg)
        gbuf[part, x_lo, z] = g_ref[at, :]
    ring_step(g_rings, 0)
    for part in range(G_PARTS):
        g_beside(part).start()
        pending.append(g_beside(part).wait_send)
    loads[1].wait()
    loads[2].wait()
    loop(4 * ny - 1, lambda i: r_out(i + 1).start())
    r_relay(0, True)[1].start()
    pending.append(lambda: loop(4 * ny - 1, lambda i: r_out(i + 1).wait_send()))
    pending.append(lambda: loop(4 * ny, lambda i: r_relay(i, True)[1].wait_send()))

    g_steps, l_steps = len(g_rings[0].hops), len(l_rings[0].hops)
    relayed, l_done = 1, 0
    for k in range(g_steps):
        if k > 0:
            ring_step(g_rings, k)
        if k >= LAG and l_done < l_steps:
            ring_step(l_rings, l_done)
            l_done += 1
        if k >= min(RELAY_AT, g_steps - 1):
            left = g_steps - k
            upto = relayed + (4 * ny - relayed + left - 1) // left
            lax.fori_loop(relayed, upto, lambda i, carry: (r_pass(i), carry)[1], 0)
            relayed = upto
    loop(4 * ny, lambda i: r_relay(i, False)[1].wait_recv())

    def p_out(i, part):
        hi, dy = lax.rem(1 - x_hi + lax.div(i, ny), 2), lax.rem(i + 2, ny)
        is_self = diagonal & (hi == x_hi) & (dy == 0)
        to = device(hi, lax.rem(y + dy, ny), c, x_hi, z)
        slot = pbuf.at[y * 2 + c, x_lo, part]
        return is_self, copy(ptile.at[part], slot, p_s.at[hi, dy, part], p_r.at[x_lo, y, part], to)

    for part in range(G_PARTS):
        for ring in g_rings:
            ring.finish((2 * part, 2 * part + 1))
        g_beside(part).wait_recv()
        partial = jnp.zeros((hg, 2 * tc), jnp.float32)
        for hi in range(2):
            for b in range(2 * ny):
                left = jnp.concatenate(
                    [gbuf[part, hi, b * ratio + k] for k in range(ratio)], axis=1
                )
                right = jnp.concatenate([rbuf[hi, 0, b], rbuf[hi, 1, b]], axis=1)
                partial += dot(left, right, 1, 0)
        ptile[part] = partial.astype(bf16)

        def p_start(i):
            is_self, send = p_out(i, part)
            pl.when(~is_self)(send.start)

        loop(2 * ny, p_start)

    def p_sent(i):
        for part in range(G_PARTS):
            is_self, send = p_out(i, part)
            pl.when(~is_self)(send.wait_send)

    pending.append(lambda: loop(2 * ny, p_sent))

    @pl.when(diagonal)
    def _():
        pbuf[y * 2 + c, x_lo] = ptile[...]

    for k in range(l_done, l_steps):
        ring_step(l_rings, k)
    for ring in l_rings:
        ring.finish(l_all)

    def share_l(yy):
        rows = pl.ds((2 * yy + sib) * ratio, ratio)
        return copy(lbuf.at[rows], lsib.at[yy], lsib_s.at[yy], lsib_r.at[yy], sibling)

    def p_relay(dy, lo, part, own):
        yy = lax.rem(y + dy, ny)
        slot = pbuf.at[yy * 2 + (c if own else sib), lo, part]
        is_self = diagonal & (lo == x_lo) & (dy == 0)
        arrive = copy(slot, slot, p_s.at[0, 0, part], p_r.at[lo, yy, part], sibling)
        at = (lo, yy, part)
        return is_self, arrive, copy(slot, slot, psib_s.at[at], psib_r.at[at], sibling)

    partial = jnp.zeros((tr, 2 * tc), jnp.float32)

    def rotate(partial, dy, core):
        block = lax.rem(y + dy, ny) * 2 + core
        left = lbuf[pl.ds(block * ratio, ratio)].reshape(tr, tr)
        return partial + dot(left, pbuf[block].reshape(tr, 2 * tc), 0, 0)

    for part in range(G_PARTS):
        for dy in range(ny):
            for lo in range(2):
                is_self, arrive, send = p_relay(dy, lo, part, True)
                pl.when(~is_self)(arrive.wait_recv)
                send.start()
            if part == G_PARTS - 1:
                partial = rotate(partial, dy, c)
    for dy in range(ny):
        for lo in range(2):
            for part in range(G_PARTS):
                p_relay(dy, lo, part, False)[2].wait_recv()
        partial = rotate(partial, dy, sib)

    def p_relayed(i):
        for part in range(G_PARTS):
            p_relay(lax.rem(i, ny), lax.div(i, ny), part, True)[2].wait_send()

    pending.append(lambda: loop(2 * ny, p_relayed))
    first, second = partial[:, :tc], partial[:, tc:]
    xsend[...] = jnp.where(x_lo == 0, second, first).astype(bf16)
    swap = copy(xsend, xrecv, x_s.at[1], x_r.at[1], beside)
    swap.start()
    loop(ny, lambda yy: share_l(yy).start())
    for load in loads[3:]:
        load.wait()
    mine = jnp.where(x_lo == 0, first, second)
    swap.wait_recv()
    pending.append(swap.wait_send)
    pending.append(lambda: loop(ny, lambda yy: share_l(yy).wait_send()))
    rotated = mine + xrecv[...].astype(jnp.float32)
    new_first = beta_one * m1_ref[...] + (1.0 - beta_one) * rotated
    new_second = beta_two * m2_ref[...] + (1.0 - beta_two) * rotated * rotated
    first_hat = new_first / (1.0 - beta_one**step_count)
    second_hat = new_second / (1.0 - beta_two**step_count)
    nbuf[c, x_lo] = (first_hat / (jnp.sqrt(second_hat) + epsilon)).astype(bf16)

    def share_n(k, to, core, lo):
        slot = nbuf.at[core, lo]
        return copy(nbuf.at[c, x_lo], slot, n_s.at[k], n_r.at[k], to)

    targets = (beside, beside_sib, sibling)
    origins = ((c, 1 - x_lo), (sib, 1 - x_lo), (sib, x_lo))
    for k in range(3):
        share_n(k, targets[k], c, x_lo).start()
    rot_ref[...] = rotated
    saves = [
        pltpu.make_async_copy(rot_ref, rot_hbm, out_sem.at[0]),
        pltpu.make_async_copy(full_ref, full_hbm, out_sem.at[1]),
    ]
    saves[0].start()
    pending.append(saves[0].wait)
    loop(ny, lambda yy: share_l(yy).wait_recv())
    for k in range(3):
        share_n(k, targets[k], *origins[k]).wait_recv()
        pending.append(share_n(k, targets[k], c, x_lo).wait_send)

    def q_out(dy, half, part):
        yy = lax.rem(y + dy, ny)
        is_self = diagonal & (half == x_lo) & (dy == 0)
        return is_self, copy(
            qsend.at[dy, half, part],
            qrecv.at[x_hi, y, part],
            q_s.at[dy, half, part],
            q_r.at[x_hi, y, part],
            device(x_lo, yy, c, half, z),
        )

    def q_start(dy, half, part):
        is_self, send = q_out(dy, half, part)
        pl.when(~is_self)(send.start)

    own_n = jnp.concatenate([nbuf[c, 0], nbuf[c, 1]], axis=1)
    sib_n = jnp.concatenate([nbuf[sib, 0], nbuf[sib, 1]], axis=1)
    for step in range(ny):
        dy = (step + 1) % ny
        yy = lax.rem(y + dy, ny)
        own_l = lbuf[pl.ds((2 * yy + c) * ratio, ratio)].reshape(tr, tr)
        sib_l = lsib[yy].reshape(tr, tr)
        block = (dot(own_l, own_n, 1, 0) + dot(sib_l, sib_n, 1, 0)).astype(bf16)
        for half in range(2):
            for part in range(PARTS):
                at = half * hr + part * hp
                qsend[dy, half, part] = block[at : at + hp]
            q_start(dy, half, 0)
    for part in range(1, PARTS):
        for step in range(ny):
            for half in range(2):
                q_start((step + 1) % ny, half, part)

    @pl.when(diagonal)
    def _():
        qrecv[x_hi, y] = qsend[0, x_lo]

    def q_sum(part):
        total = jnp.zeros((hp, 2 * tc), jnp.float32)
        for dy in range(ny):
            yy = lax.rem(y + dy, ny)
            for hi in range(2):
                is_self = diagonal & (hi == x_hi) & (dy == 0)
                slot = qrecv.at[hi, yy, part]
                arrive = copy(slot, slot, q_s.at[0, 0, part], q_r.at[hi, yy, part], beside)
                pl.when(~is_self)(arrive.wait_recv)
                total += qrecv[hi, yy, part].astype(jnp.float32)
        return total.astype(bf16)

    def q_sent(i):
        for part in range(PARTS):
            is_self, send = q_out(lax.rem(i, ny), lax.div(i, ny), part)
            pl.when(~is_self)(send.wait_send)

    pending.append(lambda: loop(2 * ny, q_sent))

    q = [None] * PARTS

    def u_own(away, ch):
        d = lax.rem(z + away + nz, nz)
        hi = x_lo if ch % 2 == 0 else 1 - x_lo
        rows = pl.ds(pl.multiple_of(lax.rem(d, ratio) * tc, tc), tc)
        at = lax.div(d, ratio)
        right = jnp.concatenate([rbuf[hi, 0, at, rows], rbuf[hi, 1, at, rows]], axis=1)
        return dot(q[ch // 2], right, 1, 1)

    own_u, other_u = range(0, 2 * PARTS, 2), range(1, 2 * PARTS, 2)
    u_rings = [
        Scatter(z, nz, 1, U_UP, far_up, own_u, u_own, uo_up, ui_up, u_us, u_ur, along),
        Scatter(z, nz, -1, U_DN, far_dn, own_u, u_own, uo_dn, ui_dn, u_ds, u_dr, along),
        Scatter(z, nz, -1, U_UP, far_up, other_u, u_own, uo_dn, ui_dn, u_ds, u_dr, along),
        Scatter(z, nz, 1, U_DN, far_dn, other_u, u_own, uo_up, ui_up, u_us, u_ur, along),
    ]

    def u_beside(part):
        return copy(uo_x.at[part], ui_x.at[part], x_s.at[2 + part], x_r.at[2 + part], beside)

    first_step = len(u_rings[0].hops) - 1
    for k in range(first_step, -1, -1):
        for part in range(PARTS):
            if k == first_step:
                q[part] = q_sum(part)
            for ch in (2 * part + 1, 2 * part):
                for ring in u_rings:
                    ring.far(k, ch)
                for ring in u_rings:
                    ring.near(k, ch)
            if k == first_step:
                uo_x[part] = u_own(0, 2 * part + 1).astype(bf16)
                u_beside(part).start()

    for part in range(PARTS):
        own = u_own(0, 2 * part)
        u_beside(part).wait_recv()
        for which, total, ch in (
            (1 - x_lo, ui_x[part].astype(jnp.float32), 2 * part + 1),
            (x_lo, own, 2 * part),
        ):
            for ring in u_rings:
                total = ring.arrived(0, ch, total)
            rows = pl.ds(pl.multiple_of(which * hr + part * hp, hp), hp)
            full_ref[rows, :] = total
        pending.append(u_beside(part).wait_send)
    saves[1].start()
    pending.append(saves[1].wait)
    pending += [ring.sent for ring in u_rings]

    for wait in pending:
        wait()


def on_device(n_row, n_col, gradient, left_basis, right_basis, first_moment, second_moment, weight):
    ny, nz = n_row // 4, n_col // 2
    tr, tc = gradient.shape
    up = nz // 2
    bf16, f32 = jnp.bfloat16, jnp.float32
    ratio, hr = tr // tc, tr // 2
    hp, hg = hr // PARTS, hr // G_PARTS
    dma = pltpu.SemaphoreType.DMA
    f32_tile = jax.ShapeDtypeStruct((tr, tc), f32)
    anywhere = pl.BlockSpec(memory_space=pl.ANY)

    def ring(pieces):
        return [dma((pieces, up))] * 4

    full_update, rotated = pl.pallas_call(
        functools.partial(kernel, ny, nz, tr, tc),
        out_shape=[f32_tile, f32_tile],
        in_specs=[anywhere] * 5,
        out_specs=[anywhere] * 2,
        scratch_shapes=[
            pltpu.VMEM((tr, tc), bf16),
            pltpu.VMEM((tr, tc), f32),
            pltpu.VMEM((tr, tc), f32),
            pltpu.VMEM((tr, tc), f32),
            pltpu.VMEM((tr, tc), f32),
            pltpu.VMEM((G_PARTS, 2, nz, hg, tc), bf16),
            pltpu.VMEM((nz, tc, tr), bf16),
            pltpu.VMEM((ny, ratio, tc, tr), bf16),
            pltpu.VMEM((2, 2, 2 * ny, tr, tc), bf16),
            pltpu.VMEM((G_PARTS, hg, 2 * tc), bf16),
            pltpu.VMEM((2 * ny, 2, G_PARTS, hg, 2 * tc), bf16),
            pltpu.VMEM((tr, tc), bf16),
            pltpu.VMEM((tr, tc), bf16),
            pltpu.VMEM((2, 2, tr, tc), bf16),
            pltpu.VMEM((ny, 2, PARTS, hp, 2 * tc), bf16),
            pltpu.VMEM((2, ny, PARTS, hp, 2 * tc), bf16),
            pltpu.VMEM((2 * PARTS, up, hp, tc), bf16),
            pltpu.VMEM((2 * PARTS, up, hp, tc), bf16),
            pltpu.VMEM((2 * PARTS, up, hp, tc), bf16),
            pltpu.VMEM((2 * PARTS, up, hp, tc), bf16),
            pltpu.VMEM((PARTS, hp, tc), bf16),
            pltpu.VMEM((PARTS, hp, tc), bf16),
            dma((5,)),
            dma((2,)),
        ]
        + ring(2 * G_PARTS)
        + ring(L_PARTS)
        + ring(2 * PARTS)
        + [dma((4 * ny,)), dma((4, ny)), dma((4, ny)), dma((4, ny))]
        + [dma((2, ny, G_PARTS))] * 4
        + [dma((ny, 2, PARTS)), dma((2, ny, PARTS))]
        + [dma((ny,)), dma((ny,)), dma((2 + PARTS + G_PARTS,)), dma((2 + PARTS + G_PARTS,)), dma((3,)), dma((3,))],
        compiler_params=pltpu.CompilerParams(
            collective_id=0, has_side_effects=True, vmem_limit_bytes=60 * 2**20
        ),
    )(gradient, left_basis, right_basis, first_moment, second_moment)
    new_first = beta_one * first_moment + (1.0 - beta_one) * rotated
    new_second = beta_two * second_moment + (1.0 - beta_two) * rotated * rotated
    update = full_update.astype(bf16)
    new_weight = weight - learn_rate * (full_update + weight_decay * weight)
    return new_weight, update, new_first, new_second


def solution(mesh):
    spec = P("row", "col")
    return jax.shard_map(
        functools.partial(on_device, mesh.shape["row"], mesh.shape["col"]),
        mesh=mesh,
        in_specs=(spec, P("col", "row"), spec, spec, spec, spec),
        out_specs=(spec,) * 4,
        check_vma=False,
    )
```

```python
import functools

import jax
import jax.numpy as jnp
from jax import lax
from jax.experimental import pallas as pl
from jax.experimental.pallas import tpu as pltpu
from jax.sharding import PartitionSpec as P

beta_one = 0.9
beta_two = 0.95
epsilon = 1e-08
learn_rate = 0.0003
weight_decay = 0.1
step_count = 20.0

MESH = pl.DeviceIdType.MESH
G_UP, G_DN = (2, 2, 2, 2), (2, 2, 2, 1)
L_UP, L_DN = (1, 1, 1, 1, 1, 1, 1, 1), (1, 1, 1, 1, 1, 1, 1)
U_UP, U_DN = (2, 2, 2, 2), (2, 2, 2, 1)
LAG = 0
PARTS = 2
G_PARTS = 1
RELAY_AT = 3
L_PARTS = 2


def dot(left, right, left_dim, right_dim):
    return lax.dot_general(
        left,
        right,
        (((left_dim,), (right_dim,)), ((), ())),
        preferred_element_type=jnp.float32,
    )


def loop(n, body):
    lax.fori_loop(0, n, lambda i, carry: (body(i), carry)[1], 0)


def copy(src, dst, send, recv, to):
    return pltpu.make_async_remote_copy(
        src_ref=src, dst_ref=dst, send_sem=send, recv_sem=recv,
        device_id=to, device_id_type=MESH,
    )


def hops(distance, wanted):
    out = []
    for hop in wanted:
        out.append(min(hop, distance - sum(out)))
    return [hop for hop in out if hop > 0]


class Gather:
    def __init__(self, z, nz, sign, hop, distance, pieces, part, first, send, recv, at):
        self.z, self.nz, self.sign, self.pieces = z, nz, sign, tuple(pieces)
        self.part, self.first, self.send, self.recv, self.at = part, first, send, recv, at
        self.hops = hops(distance, hop)
        self.stops = [sum(self.hops[:k]) for k in range(len(self.hops) + 1)]

    def piece(self, k, off, ch, sender):
        i = self.stops[k] + off - 1
        away = self.stops[k] + (0 if sender else off)
        tile = self.part(lax.rem(self.z - self.sign * away + 2 * self.nz, self.nz), ch)
        src, dst, other = tile, tile, False
        if k == 0 and sender:
            src, dst, other = self.first(ch)
        to = self.at(lax.rem(self.z + self.sign * off + self.nz, self.nz), other)
        return copy(src, dst, self.send.at[ch, i], self.recv.at[ch, i], to)

    def step(self, k, ch):
        if k < len(self.hops):
            if k > 0:
                self.piece(k - 1, self.hops[k - 1], ch, False).wait_recv()
            for off in range(self.hops[k], 0, -1):
                self.piece(k, off, ch, True).start()

    def finish(self, pieces):
        last = len(self.hops) - 1
        for k, hop in enumerate(self.hops):
            for off in range(1, hop + (k == last)):
                for ch in self.pieces:
                    if ch in pieces:
                        self.piece(k, off, ch, False).wait_recv()

    def sent(self):
        for k, hop in enumerate(self.hops):
            for off in range(1, hop + 1):
                for ch in self.pieces:
                    self.piece(k, off, ch, True).wait_send()


class Scatter:
    def __init__(self, z, nz, sign, hop, distance, pieces, own, out, into, send, recv, at):
        self.z, self.nz, self.sign, self.pieces = z, nz, sign, tuple(pieces)
        self.own, self.out, self.into, self.send, self.recv, self.at = own, out, into, send, recv, at
        self.hops = hops(distance, hop)
        self.stops = [sum(self.hops[:k]) for k in range(len(self.hops) + 1)]

    def piece(self, k, off, ch):
        i = self.stops[k] + off - 1
        to = self.at(lax.rem(self.z + self.sign * off + self.nz, self.nz), k == 0 and ch % 2 == 1)
        return copy(self.out.at[ch, i], self.into.at[ch, i], self.send.at[ch, i], self.recv.at[ch, i], to)

    def arrived(self, k, ch, total):
        if k < len(self.hops) and ch in self.pieces:
            for off in range(1, self.hops[k] + 1):
                self.piece(k, off, ch).wait_recv()
                total += self.into[ch, self.stops[k] + off - 1].astype(jnp.float32)
        return total

    def far(self, k, ch):
        if k < len(self.hops) and ch in self.pieces:
            stop = self.stops[k + 1]
            total = self.arrived(k + 1, ch, self.own(self.sign * stop, ch))
            self.out[ch, stop - 1] = total.astype(jnp.bfloat16)
            self.piece(k, self.hops[k], ch).start()

    def near(self, k, ch):
        if k < len(self.hops) and ch in self.pieces:
            for off in range(1, self.hops[k]):
                stop = self.stops[k] + off
                self.out[ch, stop - 1] = self.own(self.sign * stop, ch).astype(jnp.bfloat16)
                self.piece(k, off, ch).start()

    def sent(self):
        for k, hop in enumerate(self.hops):
            for off in range(1, hop + 1):
                for ch in self.pieces:
                    self.piece(k, off, ch).wait_send()


def kernel(
    ny, nz, tr, tc,
    g_hbm, l_hbm, r_hbm, m1_hbm, m2_hbm,
    full_hbm, rot_hbm,
    g_ref, m1_ref, m2_ref, full_ref, rot_ref,
    gbuf, lbuf, lsib, rbuf, ptile, pbuf, xsend, xrecv, nbuf, qsend, qrecv,
    uo_up, ui_up, uo_dn, ui_dn, uo_x, ui_x,
    in_sem, out_sem,
    g_us, g_ur, g_ds, g_dr, l_us, l_ur, l_ds, l_dr, u_us, u_ur, u_ds, u_dr,
    r_s, r_r, rsib_s, rsib_r, p_s, p_r, psib_s, psib_r, q_s, q_r,
    lsib_s, lsib_r, x_s, x_r, n_s, n_r,
):
    bf16 = jnp.bfloat16
    ratio, hr = tr // tc, tr // 2
    hp = hr // PARTS
    far_up, far_dn = nz // 2, nz - 1 - nz // 2
    row, col = lax.axis_index("row"), lax.axis_index("col")
    x_hi, y, c = lax.div(row, 2 * ny), lax.rem(lax.div(row, 2), ny), lax.rem(row, 2)
    x_lo, z = lax.div(col, nz), lax.rem(col, nz)
    sib = 1 - c
    diagonal = x_hi == x_lo

    own_r = rbuf.at[x_hi, x_lo, y * 2 + c]
    sources = (g_hbm, l_hbm, r_hbm, m1_hbm, m2_hbm)
    places = (g_ref, lbuf.at[z], own_r, m1_ref, m2_ref)
    loads = [pltpu.make_async_copy(s, d, in_sem.at[i]) for i, (s, d) in enumerate(zip(sources, places))]
    for load in loads:
        load.start()

    def device(x_hi, y, c, x_lo, z):
        return ((x_hi * ny + y) * 2 + c, x_lo * nz + z)

    def along(to_z, other):
        return device(x_hi, y, c, 1 - x_lo if other else x_lo, to_z)

    sibling = device(x_hi, y, sib, x_lo, z)
    beside = device(x_hi, y, c, 1 - x_lo, z)
    beside_sib = device(x_hi, y, sib, 1 - x_lo, z)

    barrier = pltpu.get_barrier_semaphore()

    def greet(to):
        pl.semaphore_signal(barrier, inc=1, device_id=to, device_id_type=MESH)

    def in_plane(i):
        peer = lax.rem(x_hi * 2 + x_lo + lax.div(i, ny), 4)
        return lax.div(peer, 2), lax.rem(peer, 2), lax.rem(y + lax.rem(i, ny), ny)

    def greet_plane(i):
        hi, lo, yy = in_plane(i + 1)
        greet(device(hi, yy, c, lo, z))

    near = sorted({k % nz for k in (1, -1, 2, -2)} - {0})
    for k in near:
        for other in (False, True):
            greet(along(lax.rem(z + k, nz), other))
    greet(sibling)
    greet(beside_sib)
    loop(4 * ny - 1, greet_plane)
    pl.semaphore_wait(barrier, 2 * len(near) + 2 + 4 * ny - 1)

    hg = hr // G_PARTS

    def g_part(tile, ch):
        return gbuf.at[ch // 2, x_lo if ch % 2 == 0 else 1 - x_lo, tile]

    def g_rows(which, part):
        return g_ref.at[pl.ds(pl.multiple_of(which * hr + part * hg, hg), hg)]

    def g_first(ch):
        which = x_lo if ch % 2 == 0 else 1 - x_lo
        return g_rows(which, ch // 2), gbuf.at[ch // 2, x_lo, z], ch % 2 == 1

    lrows = tc // L_PARTS

    def l_part(tile, ch):
        return lbuf.at[tile, pl.ds(ch * lrows, lrows)]

    def l_first(ch):
        return l_part(z, ch), l_part(z, ch), False

    own_g, other_g = range(0, 2 * G_PARTS, 2), range(1, 2 * G_PARTS, 2)
    g_rings = [
        Gather(z, nz, 1, G_UP, far_up, own_g, g_part, g_first, g_us, g_ur, along),
        Gather(z, nz, -1, G_DN, far_dn, own_g, g_part, g_first, g_ds, g_dr, along),
        Gather(z, nz, -1, G_UP, far_up, other_g, g_part, g_first, g_ds, g_dr, along),
        Gather(z, nz, 1, G_DN, far_dn, other_g, g_part, g_first, g_us, g_ur, along),
    ]
    l_all = range(L_PARTS)
    l_rings = [
        Gather(z, nz, 1, L_UP, far_up, l_all, l_part, l_first, l_us, l_ur, along),
        Gather(z, nz, -1, L_DN, far_dn, l_all, l_part, l_first, l_ds, l_dr, along),
    ]

    pending = [ring.sent for ring in g_rings + l_rings]

    def ring_step(rings, k):
        for ch in sorted({ch for ring in rings for ch in ring.pieces}):
            for ring in rings:
                if ch in ring.pieces:
                    ring.step(k, ch)

    def g_beside(part):
        sem = 2 + PARTS + part
        return copy(
            g_rows(1 - x_lo, part), gbuf.at[part, x_lo, z], x_s.at[sem], x_r.at[sem], beside
        )

    def r_out(i):
        hi, lo, yy = in_plane(i)
        return copy(
            own_r, own_r, r_s.at[i], r_r.at[x_hi * 2 + x_lo, y], device(hi, yy, c, lo, z)
        )

    def r_relay(i, own):
        hi, lo, yy = in_plane(i)
        slot = rbuf.at[hi, lo, yy * 2 + (c if own else sib)]
        at = (hi * 2 + lo, yy)
        send = copy(slot, slot, rsib_s.at[at], rsib_r.at[at], sibling)
        arrive = copy(slot, slot, r_s.at[0], r_r.at[at], sibling)
        return arrive, send

    def r_pass(i):
        arrive, send = r_relay(i, True)
        arrive.wait_recv()
        send.start()

    loads[0].wait()
    for part in range(G_PARTS):
        at = pl.ds(pl.multiple_of(x_lo * hr + part * hg, hg), hg)
        gbuf[part, x_lo, z] = g_ref[at, :]
    ring_step(g_rings, 0)
    for part in range(G_PARTS):
        g_beside(part).start()
        pending.append(g_beside(part).wait_send)
    loads[1].wait()
    loads[2].wait()
    loop(4 * ny - 1, lambda i: r_out(i + 1).start())
    r_relay(0, True)[1].start()
    pending.append(lambda: loop(4 * ny - 1, lambda i: r_out(i + 1).wait_send()))
    pending.append(lambda: loop(4 * ny, lambda i: r_relay(i, True)[1].wait_send()))

    g_steps, l_steps = len(g_rings[0].hops), len(l_rings[0].hops)
    relayed, l_done = 1, 0
    for k in range(g_steps):
        if k > 0:
            ring_step(g_rings, k)
        if k >= LAG and l_done < l_steps:
            ring_step(l_rings, l_done)
            l_done += 1
        if k >= min(RELAY_AT, g_steps - 1):
            left = g_steps - k
            upto = relayed + (4 * ny - relayed + left - 1) // left
            lax.fori_loop(relayed, upto, lambda i, carry: (r_pass(i), carry)[1], 0)
            relayed = upto
    loop(4 * ny, lambda i: r_relay(i, False)[1].wait_recv())

    def p_out(i, part):
        hi, dy = lax.rem(1 - x_hi + lax.div(i, ny), 2), lax.rem(i + 2, ny)
        is_self = diagonal & (hi == x_hi) & (dy == 0)
        to = device(hi, lax.rem(y + dy, ny), c, x_hi, z)
        slot = pbuf.at[y * 2 + c, x_lo, part]
        return is_self, copy(ptile.at[part], slot, p_s.at[hi, dy, part], p_r.at[x_lo, y, part], to)

    for part in range(G_PARTS):
        for ring in g_rings:
            ring.finish((2 * part, 2 * part + 1))
        g_beside(part).wait_recv()
        partial = jnp.zeros((hg, 2 * tc), jnp.float32)
        for hi in range(2):
            for b in range(2 * ny):
                left = jnp.concatenate(
                    [gbuf[part, hi, b * ratio + k] for k in range(ratio)], axis=1
                )
                right = jnp.concatenate([rbuf[hi, 0, b], rbuf[hi, 1, b]], axis=1)
                partial += dot(left, right, 1, 0)
        ptile[part] = partial.astype(bf16)

        def p_start(i):
            is_self, send = p_out(i, part)
            pl.when(~is_self)(send.start)

        loop(2 * ny, p_start)

    def p_sent(i):
        for part in range(G_PARTS):
            is_self, send = p_out(i, part)
            pl.when(~is_self)(send.wait_send)

    pending.append(lambda: loop(2 * ny, p_sent))

    @pl.when(diagonal)
    def _():
        pbuf[y * 2 + c, x_lo] = ptile[...]

    for k in range(l_done, l_steps):
        ring_step(l_rings, k)
    for ring in l_rings:
        ring.finish(l_all)

    def share_l(yy):
        rows = pl.ds((2 * yy + sib) * ratio, ratio)
        return copy(lbuf.at[rows], lsib.at[yy], lsib_s.at[yy], lsib_r.at[yy], sibling)

    def p_relay(dy, lo, part, own):
        yy = lax.rem(y + dy, ny)
        slot = pbuf.at[yy * 2 + (c if own else sib), lo, part]
        is_self = diagonal & (lo == x_lo) & (dy == 0)
        arrive = copy(slot, slot, p_s.at[0, 0, part], p_r.at[lo, yy, part], sibling)
        at = (lo, yy, part)
        return is_self, arrive, copy(slot, slot, psib_s.at[at], psib_r.at[at], sibling)

    partial = jnp.zeros((tr, 2 * tc), jnp.float32)

    def rotate(partial, dy, core):
        block = lax.rem(y + dy, ny) * 2 + core
        left = lbuf[pl.ds(block * ratio, ratio)].reshape(tr, tr)
        return partial + dot(left, pbuf[block].reshape(tr, 2 * tc), 0, 0)

    for part in range(G_PARTS):
        for dy in range(ny):
            for lo in range(2):
                is_self, arrive, send = p_relay(dy, lo, part, True)
                pl.when(~is_self)(arrive.wait_recv)
                send.start()
            if part == G_PARTS - 1:
                partial = rotate(partial, dy, c)
    for dy in range(ny):
        for lo in range(2):
            for part in range(G_PARTS):
                p_relay(dy, lo, part, False)[2].wait_recv()
        partial = rotate(partial, dy, sib)

    def p_relayed(i):
        for part in range(G_PARTS):
            p_relay(lax.rem(i, ny), lax.div(i, ny), part, True)[2].wait_send()

    pending.append(lambda: loop(2 * ny, p_relayed))
    first, second = partial[:, :tc], partial[:, tc:]
    xsend[...] = jnp.where(x_lo == 0, second, first).astype(bf16)
    swap = copy(xsend, xrecv, x_s.at[1], x_r.at[1], beside)
    swap.start()
    loop(ny, lambda yy: share_l(yy).start())
    for load in loads[3:]:
        load.wait()
    mine = jnp.where(x_lo == 0, first, second)
    swap.wait_recv()
    pending.append(swap.wait_send)
    pending.append(lambda: loop(ny, lambda yy: share_l(yy).wait_send()))
    rotated = mine + xrecv[...].astype(jnp.float32)
    new_first = beta_one * m1_ref[...] + (1.0 - beta_one) * rotated
    new_second = beta_two * m2_ref[...] + (1.0 - beta_two) * rotated * rotated
    first_hat = new_first / (1.0 - beta_one**step_count)
    second_hat = new_second / (1.0 - beta_two**step_count)
    nbuf[c, x_lo] = (first_hat / (jnp.sqrt(second_hat) + epsilon)).astype(bf16)

    def share_n(k, to, core, lo):
        slot = nbuf.at[core, lo]
        return copy(nbuf.at[c, x_lo], slot, n_s.at[k], n_r.at[k], to)

    targets = (beside, beside_sib, sibling)
    origins = ((c, 1 - x_lo), (sib, 1 - x_lo), (sib, x_lo))
    for k in range(3):
        share_n(k, targets[k], c, x_lo).start()
    rot_ref[...] = rotated
    saves = [
        pltpu.make_async_copy(rot_ref, rot_hbm, out_sem.at[0]),
        pltpu.make_async_copy(full_ref, full_hbm, out_sem.at[1]),
    ]
    saves[0].start()
    pending.append(saves[0].wait)
    loop(ny, lambda yy: share_l(yy).wait_recv())
    for k in range(3):
        share_n(k, targets[k], *origins[k]).wait_recv()
        pending.append(share_n(k, targets[k], c, x_lo).wait_send)

    def q_out(dy, half, part):
        yy = lax.rem(y + dy, ny)
        is_self = diagonal & (half == x_lo) & (dy == 0)
        return is_self, copy(
            qsend.at[dy, half, part],
            qrecv.at[x_hi, y, part],
            q_s.at[dy, half, part],
            q_r.at[x_hi, y, part],
            device(x_lo, yy, c, half, z),
        )

    def q_start(dy, half, part):
        is_self, send = q_out(dy, half, part)
        pl.when(~is_self)(send.start)

    own_n = jnp.concatenate([nbuf[c, 0], nbuf[c, 1]], axis=1)
    sib_n = jnp.concatenate([nbuf[sib, 0], nbuf[sib, 1]], axis=1)
    for step in range(ny):
        dy = (step + 1) % ny
        yy = lax.rem(y + dy, ny)
        own_l = lbuf[pl.ds((2 * yy + c) * ratio, ratio)].reshape(tr, tr)
        sib_l = lsib[yy].reshape(tr, tr)
        block = (dot(own_l, own_n, 1, 0) + dot(sib_l, sib_n, 1, 0)).astype(bf16)
        for half in range(2):
            for part in range(PARTS):
                at = half * hr + part * hp
                qsend[dy, half, part] = block[at : at + hp]
            q_start(dy, half, 0)
    for part in range(1, PARTS):
        for step in range(ny):
            for half in range(2):
                q_start((step + 1) % ny, half, part)

    @pl.when(diagonal)
    def _():
        qrecv[x_hi, y] = qsend[0, x_lo]

    def q_sum(part):
        total = jnp.zeros((hp, 2 * tc), jnp.float32)
        for dy in range(ny):
            yy = lax.rem(y + dy, ny)
            for hi in range(2):
                is_self = diagonal & (hi == x_hi) & (dy == 0)
                slot = qrecv.at[hi, yy, part]
                arrive = copy(slot, slot, q_s.at[0, 0, part], q_r.at[hi, yy, part], beside)
                pl.when(~is_self)(arrive.wait_recv)
                total += qrecv[hi, yy, part].astype(jnp.float32)
        return total.astype(bf16)

    def q_sent(i):
        for part in range(PARTS):
            is_self, send = q_out(lax.rem(i, ny), lax.div(i, ny), part)
            pl.when(~is_self)(send.wait_send)

    pending.append(lambda: loop(2 * ny, q_sent))

    q = [None] * PARTS

    def u_own(away, ch):
        d = lax.rem(z + away + nz, nz)
        hi = x_lo if ch % 2 == 0 else 1 - x_lo
        rows = pl.ds(pl.multiple_of(lax.rem(d, ratio) * tc, tc), tc)
        at = lax.div(d, ratio)
        right = jnp.concatenate([rbuf[hi, 0, at, rows], rbuf[hi, 1, at, rows]], axis=1)
        return dot(q[ch // 2], right, 1, 1)

    own_u, other_u = range(0, 2 * PARTS, 2), range(1, 2 * PARTS, 2)
    u_rings = [
        Scatter(z, nz, 1, U_UP, far_up, own_u, u_own, uo_up, ui_up, u_us, u_ur, along),
        Scatter(z, nz, -1, U_DN, far_dn, own_u, u_own, uo_dn, ui_dn, u_ds, u_dr, along),
        Scatter(z, nz, -1, U_UP, far_up, other_u, u_own, uo_dn, ui_dn, u_ds, u_dr, along),
        Scatter(z, nz, 1, U_DN, far_dn, other_u, u_own, uo_up, ui_up, u_us, u_ur, along),
    ]

    def u_beside(part):
        return copy(uo_x.at[part], ui_x.at[part], x_s.at[2 + part], x_r.at[2 + part], beside)

    first_step = len(u_rings[0].hops) - 1
    for k in range(first_step, -1, -1):
        for part in range(PARTS):
            if k == first_step:
                q[part] = q_sum(part)
            for ch in (2 * part + 1, 2 * part):
                for ring in u_rings:
                    ring.far(k, ch)
                for ring in u_rings:
                    ring.near(k, ch)
            if k == first_step:
                uo_x[part] = u_own(0, 2 * part + 1).astype(bf16)
                u_beside(part).start()

    for part in range(PARTS):
        own = u_own(0, 2 * part)
        u_beside(part).wait_recv()
        for which, total, ch in (
            (1 - x_lo, ui_x[part].astype(jnp.float32), 2 * part + 1),
            (x_lo, own, 2 * part),
        ):
            for ring in u_rings:
                total = ring.arrived(0, ch, total)
            rows = pl.ds(pl.multiple_of(which * hr + part * hp, hp), hp)
            full_ref[rows, :] = total
        pending.append(u_beside(part).wait_send)
    saves[1].start()
    pending.append(saves[1].wait)
    pending += [ring.sent for ring in u_rings]

    for wait in pending:
        wait()


def on_device(n_row, n_col, gradient, left_basis, right_basis, first_moment, second_moment, weight):
    ny, nz = n_row // 4, n_col // 2
    tr, tc = gradient.shape
    up = nz // 2
    bf16, f32 = jnp.bfloat16, jnp.float32
    ratio, hr = tr // tc, tr // 2
    hp, hg = hr // PARTS, hr // G_PARTS
    dma = pltpu.SemaphoreType.DMA
    f32_tile = jax.ShapeDtypeStruct((tr, tc), f32)
    anywhere = pl.BlockSpec(memory_space=pl.ANY)

    def ring(pieces):
        return [dma((pieces, up))] * 4

    full_update, rotated = pl.pallas_call(
        functools.partial(kernel, ny, nz, tr, tc),
        out_shape=[f32_tile, f32_tile],
        in_specs=[anywhere] * 5,
        out_specs=[anywhere] * 2,
        scratch_shapes=[
            pltpu.VMEM((tr, tc), bf16),
            pltpu.VMEM((tr, tc), f32),
            pltpu.VMEM((tr, tc), f32),
            pltpu.VMEM((tr, tc), f32),
            pltpu.VMEM((tr, tc), f32),
            pltpu.VMEM((G_PARTS, 2, nz, hg, tc), bf16),
            pltpu.VMEM((nz, tc, tr), bf16),
            pltpu.VMEM((ny, ratio, tc, tr), bf16),
            pltpu.VMEM((2, 2, 2 * ny, tr, tc), bf16),
            pltpu.VMEM((G_PARTS, hg, 2 * tc), bf16),
            pltpu.VMEM((2 * ny, 2, G_PARTS, hg, 2 * tc), bf16),
            pltpu.VMEM((tr, tc), bf16),
            pltpu.VMEM((tr, tc), bf16),
            pltpu.VMEM((2, 2, tr, tc), bf16),
            pltpu.VMEM((ny, 2, PARTS, hp, 2 * tc), bf16),
            pltpu.VMEM((2, ny, PARTS, hp, 2 * tc), bf16),
            pltpu.VMEM((2 * PARTS, up, hp, tc), bf16),
            pltpu.VMEM((2 * PARTS, up, hp, tc), bf16),
            pltpu.VMEM((2 * PARTS, up, hp, tc), bf16),
            pltpu.VMEM((2 * PARTS, up, hp, tc), bf16),
            pltpu.VMEM((PARTS, hp, tc), bf16),
            pltpu.VMEM((PARTS, hp, tc), bf16),
            dma((5,)),
            dma((2,)),
        ]
        + ring(2 * G_PARTS)
        + ring(L_PARTS)
        + ring(2 * PARTS)
        + [dma((4 * ny,)), dma((4, ny)), dma((4, ny)), dma((4, ny))]
        + [dma((2, ny, G_PARTS))] * 4
        + [dma((ny, 2, PARTS)), dma((2, ny, PARTS))]
        + [dma((ny,)), dma((ny,)), dma((2 + PARTS + G_PARTS,)), dma((2 + PARTS + G_PARTS,)), dma((3,)), dma((3,))],
        compiler_params=pltpu.CompilerParams(
            collective_id=0, has_side_effects=True, vmem_limit_bytes=60 * 2**20
        ),
    )(gradient, left_basis, right_basis, first_moment, second_moment)
    new_first = beta_one * first_moment + (1.0 - beta_one) * rotated
    new_second = beta_two * second_moment + (1.0 - beta_two) * rotated * rotated
    update = full_update.astype(bf16)
    new_weight = weight - learn_rate * (full_update + weight_decay * weight)
    return new_weight, update, new_first, new_second


def solution(mesh):
    spec = P("row", "col")
    return jax.shard_map(
        functools.partial(on_device, mesh.shape["row"], mesh.shape["col"]),
        mesh=mesh,
        in_specs=(spec, P("col", "row"), spec, spec, spec, spec),
        out_specs=(spec,) * 4,
        check_vma=False,
    )
```
